256 devices in a mesh: log: 64 (over y, z, core), pix: 4 (over x).
Axes of the slice: x: 4, y: 4, z: 8, core: 2. Of those that a mesh axis runs over, the one named last changes fastest.
Arguments:
- features: bfloat16 [1024, 1536, 128], P('log', 'pix'), may hold values from -4.5 to 4.5
- endpoint_owner: int32 [1792, 1], P('log'), may hold values from 0 to 63; in each aligned block of 28 rows (0 to 27, 28 to 55, ...) no two rows name the same one
- endpoint_frame: int32 [1792, 1], P('log'), may hold values from 0 to 15
- grad_matched: bfloat16 [896, 1536, 128], P('log', 'pix'), may hold values from -6 to 6
Outputs:
- grad_features: float32 [1024, 1536, 128], P('log', 'pix')
The draws below stay inside these ranges and needn't reach their ends.
Inputs may be any that keep to these rules, and one draw needn't show every extreme that they name: `endpoint_owner`: within the (28) rows of one device no owner is named more than 1 times, a bound that some block reaches.
All inputs are finite; a program needn't handle non-finite values.
Results may differ from the reference program's by a relative error of at most 0.0075.
Values may be sent and summed in bfloat16 or wider, within the bound.
No kernel may reach another device: no remote copies, remote signals or barrier semaphores. Data moves between devices by JAX's collectives and lax.ppermute only.
A program may use at most 128 MiB of HBM per device.

```python
import math
import jax
import jax.numpy as jnp
import numpy as np
from jax import lax

P_SIZE = 1536
C = 128
F_DEV = 16
E_DEV = 14
CAP = 1
FRAMES = 1024
EDGES = 896
ENDS = 1792
N_LOG = 64


def draw_features(key, part):
    key = jax.random.fold_in(key, 17)
    first = jax.random.fold_in(key, 0)
    values = jnp.clip(jax.random.normal(first, (FRAMES, P_SIZE, C), jnp.float32), -4.5, 4.5)
    return values.astype(jnp.bfloat16)


def plant(result, own_key, low, top_value):
    place = [jax.random.randint(jax.random.fold_in(own_key, axis), (), 0, length) for axis, length in enumerate(result.shape)]
    main_axis = result.shape.index(max(result.shape))
    neighbour = place[:main_axis] + [(place[main_axis] + 1) % result.shape[main_axis]] + place[main_axis + 1:]
    return result.at[tuple(place)].set(low).at[tuple(neighbour)].set(top_value)


def shard_levels(key, extent, pieces, low, top_value):
    gain = 1.0
    for dim, blocks in pieces:
        steps = jax.random.uniform(jax.random.fold_in(jax.random.fold_in(key, 6), dim), (blocks,), jnp.float32, low / len(pieces), top_value / len(pieces))
        gain = gain * jnp.repeat(jnp.exp(steps), extent[dim] // blocks).reshape((-1,) + (1,) * (len(extent) - 1 - dim))
    return gain


def deal_out(stream_key, own, number, rows, amount, top, limit, skew):
    sequence = jax.random.permutation(stream_key, amount)
    packed, common = load_shares(amount, rows * top, limit, skew, True), load_shares(amount, rows * top, limit, skew, False)
    places = jnp.arange(amount)

    def named(tallies, rotation):
        used = int((tallies > 0).sum())
        fixed = max(1, used // 4)
        moved = fixed + (places - fixed + rotation * (used - fixed)) % max(1, amount - fixed)
        return jnp.zeros((amount,), jnp.int32).at[sequence[jnp.where(places < fixed, places, moved)]].set(jnp.asarray(tallies, jnp.int32))

    tallies = jnp.where(number % 4 == 0, named(packed, number // 4), named(common, number - number // 4 - 1))
    mixed = jax.random.permutation(jax.random.fold_in(own, 3), amount)
    source_of, taker = mixed[0:amount // 2 * 2:2], mixed[1:amount // 2 * 2:2]
    room = jnp.minimum(tallies[source_of] - 1, limit - tallies[taker]) // 2
    room = jnp.where((source_of == sequence[0]) | (taker == sequence[0]) | (tallies[taker] == 0), 0, jnp.maximum(room, 0))
    moved = jax.random.randint(jax.random.fold_in(own, 4), (amount // 2,), 0, 1 << 20) % (room + 1)
    tallies = tallies.at[source_of].add(-moved).at[taker].add(moved)
    labels = jnp.searchsorted(jnp.cumsum(tallies), jnp.arange(rows * top), side="right").astype(jnp.int32)
    grid = labels.reshape(top, rows).T
    grid = grid[jax.random.permutation(jax.random.fold_in(own, 1), rows)]
    rotation = jax.random.randint(jax.random.fold_in(own, 2), (rows, 1), 0, top)
    return jnp.take_along_axis(grid, (jnp.arange(top)[None, :] + rotation) % top, axis=1)


def load_shares(count, total, limit, lean, full):
    portions = [(1 << 20) // math.isqrt(rank ** lean) + 1 for rank in range(1, count + 1)]
    largest = limit if full else min(limit, max(-(-total // count), total * portions[0] // sum(portions)))
    least = 1 if total - largest >= count - 1 else 0
    counts, surplus = [largest] + [least] * (count - 1), total - largest - least * (count - 1)
    while surplus > 0:
        movable = [i for i in range(1, count) if counts[i] < largest] or [i for i in range(1, count) if counts[i] < limit]
        pool, budget = sum([portions[i] for i in movable]), surplus
        for i in movable:
            extra = min(limit - counts[i], max(1, budget * portions[i] // pool), surplus)
            counts[i] = counts[i] + extra
            surplus = surplus - extra
    return np.array(counts)


def scatter_about(rng, dims, scale, bound, cuts=(), held_as=jnp.bfloat16):
    entries = scale * jax.random.normal(rng, dims, jnp.float32)
    if cuts:
        entries = entries * shard_levels(rng, dims, cuts, -0.22, 0.18)
    return jnp.clip(entries, -bound, bound).astype(held_as)


def setup_inputs(seed: int = 0) -> dict:
    key_of = jax.random.split(jax.random.key(seed), 5)
    features = draw_features(jax.random.fold_in(key_of[4], 71), 0)
    endpoint_owner_keys = jax.random.split(jax.random.fold_in(key_of[1], 1), ENDS // (2 * E_DEV))
    endpoint_owner_turns = jax.random.permutation(jax.random.fold_in(key_of[1], 3), ENDS // (2 * E_DEV))
    endpoint_owner = jax.vmap(lambda own, number: deal_out(jax.random.fold_in(key_of[1], 2), own, number, 2 * E_DEV, N_LOG, 1, CAP, 2))(endpoint_owner_keys, endpoint_owner_turns).reshape((ENDS, 1))
    endpoint_frame = plant(jax.random.randint(key_of[2], (ENDS, 1), 0, F_DEV), jax.random.fold_in(key_of[2], 1), 0, F_DEV - 1).astype(jnp.int32)
    grad_matched = scatter_about(key_of[3], (EDGES, P_SIZE, C), 1.0, 6.0, ((0, 64), (1, 4)))
    return {"features": features, "endpoint_owner": endpoint_owner, "endpoint_frame": endpoint_frame, "grad_matched": grad_matched}


def edge_backward(query, keys, cotangent):
    scale = query.shape[-1] ** -0.5
    scores = jnp.dot(query, keys.T, preferred_element_type=jnp.float32) * scale
    top = jnp.max(scores, axis=1, keepdims=True)
    expo = jnp.exp(scores - top)
    total = jnp.sum(expo, axis=1, keepdims=True)
    probs = expo / total
    probs_low = probs.astype(jnp.bfloat16)
    matched = jnp.dot(probs_low, keys, preferred_element_type=jnp.float32)
    delta = jnp.sum(cotangent.astype(jnp.float32) * matched, axis=1, keepdims=True)
    dprobs = jnp.dot(cotangent, keys.T, preferred_element_type=jnp.float32)
    dscores = (probs * (dprobs - delta)).astype(jnp.bfloat16)
    grad_query = jnp.dot(dscores, keys, preferred_element_type=jnp.float32) * scale
    grad_keys = jnp.dot(dscores.T, query, preferred_element_type=jnp.float32) * scale
    grad_keys = grad_keys + jnp.dot(probs_low.T, cotangent, preferred_element_type=jnp.float32)
    return grad_query, grad_keys


def reference(features, endpoint_owner, endpoint_frame, grad_matched):
    frame_ids = (endpoint_owner[:, 0] * F_DEV + endpoint_frame[:, 0]).astype(jnp.int32)
    pairs = frame_ids.reshape(EDGES, 2)

    def one_edge(args):
        pair, cotangent = args
        query = features[pair[0]]
        keys = features[pair[1]]
        grad_query, grad_keys = edge_backward(query, keys, cotangent)
        return grad_query.astype(jnp.bfloat16), grad_keys.astype(jnp.bfloat16)

    grad_source, grad_target = lax.map(one_edge, (pairs, grad_matched))
    grads = jnp.zeros((FRAMES, P_SIZE, C), jnp.float32)
    grads = grads.at[pairs[:, 0]].add(grad_source.astype(jnp.float32))
    grads = grads.at[pairs[:, 1]].add(grad_target.astype(jnp.float32))
    return grads
```

```python
import functools
import math

import jax
import jax.numpy as jnp
from jax import lax
from jax.experimental import pallas as pl
from jax.experimental.pallas import tpu as pltpu
from jax.sharding import PartitionSpec as P

F32 = jnp.float32
BF16 = jnp.bfloat16
LANES = 128
PAD_ID = 2047
VMEM_LIMIT = 48 * 2**20


def dot(a, b, ca, cb):
    return lax.dot_general(a, b, (((ca,), (cb,)), ((), ())), preferred_element_type=F32)


def spread_kernel(peers, piece, feat_ref, out_ref, wide):
    frames, rows, chans = feat_ref.shape
    for f in range(frames):
        wide[f * rows : (f + 1) * rows, :] = feat_ref[f].astype(F32)

    def one(d, carry):
        for k in range(piece):
            block = wide[pl.ds(k * peers + d, frames, stride=rows), :]
            out_ref[d, k * frames : (k + 1) * frames, :] = block.astype(BF16)
        return carry

    lax.fori_loop(0, peers, one, 0)


def spread(features, peers):
    frames, rows, chans = features.shape
    piece = rows // peers
    return pl.pallas_call(
        functools.partial(spread_kernel, peers, piece),
        out_shape=jax.ShapeDtypeStruct((peers, piece * frames, chans), BF16),
        in_specs=[pl.BlockSpec(memory_space=pltpu.VMEM)],
        out_specs=pl.BlockSpec(memory_space=pltpu.VMEM),
        scratch_shapes=[pltpu.VMEM((frames * rows, chans), F32)],
        compiler_params=pltpu.CompilerParams(vmem_limit_bytes=VMEM_LIMIT),
        name="spread",
    )(features)


def split_ids(ids_ref):
    ids = ids_ref[...]
    high = lax.shift_right_logical(ids, 4)
    low = ids - high * 16
    return high.astype(F32).astype(BF16), low.astype(F32).astype(BF16)


def id_column(ids_ref, part, slots):
    peers = ids_ref.shape[0]
    count = peers * slots
    high, low = split_ids(ids_ref)
    row = lax.broadcasted_iota(jnp.int32, (count, peers), 0)
    col = lax.broadcasted_iota(jnp.int32, (count, peers), 1)
    pick = (lax.div(row, slots) == col).astype(F32).astype(BF16)
    every = dot(pick, high, 1, 0) * 16.0 + dot(pick, low, 1, 0)
    row = lax.broadcasted_iota(jnp.int32, (count, LANES), 0)
    lane = lax.broadcasted_iota(jnp.int32, (count, LANES), 1)
    mine = lane == part * slots + lax.rem(row, slots)
    return jnp.sum(jnp.where(mine, every, 0.0), axis=1, keepdims=True)


def id_row(ids_ref, part, slots):
    peers = ids_ref.shape[0]
    count = peers * slots
    high, low = split_ids(ids_ref)
    row = lax.broadcasted_iota(jnp.int32, (LANES, count), 0)
    col = lax.broadcasted_iota(jnp.int32, (LANES, count), 1)
    pick = (row == part * slots + lax.rem(col, slots)).astype(F32).astype(BF16)
    every = dot(high, pick, 1, 0) * 16.0 + dot(low, pick, 1, 0)
    row = lax.broadcasted_iota(jnp.int32, (peers, count), 0)
    col = lax.broadcasted_iota(jnp.int32, (peers, count), 1)
    return jnp.sum(jnp.where(lax.div(col, slots) == row, every, 0.0), axis=0, keepdims=True)


def fetch_kernel(slots, piece, frames, held_ref, ids_ref, out_ref, table):
    part = pl.program_id(0)
    peers = held_ref.shape[0]
    total = peers * frames

    @pl.when(part == 0)
    def _():
        for k in range(piece):
            block = held_ref[:, k * frames : (k + 1) * frames, :]
            table[:, k * LANES : (k + 1) * LANES] = block.reshape(total, LANES)

    column = id_column(ids_ref, part, slots)
    count = peers * slots
    lane = lax.broadcasted_iota(jnp.int32, (count, total), 1).astype(F32)
    chosen = jnp.where(column == lane, 1.0, 0.0).astype(BF16)
    rows = dot(chosen, table[...], 1, 0)
    for pair in range(piece // 2):
        halves = [
            rows[:, (2 * pair + h) * LANES : (2 * pair + h + 1) * LANES].reshape(peers, slots, LANES)
            for h in range(2)
        ]
        both = jnp.concatenate(halves, axis=1)
        out_ref[:, pair * 2 * slots : (pair + 1) * 2 * slots, :] = both.astype(BF16)


def fetch(held, ids, parts, slots, piece, frames):
    peers = held.shape[0]
    return pl.pallas_call(
        functools.partial(fetch_kernel, slots, piece, frames),
        grid=(parts,),
        out_shape=jax.ShapeDtypeStruct((parts * peers, piece * slots, LANES), BF16),
        in_specs=[
            pl.BlockSpec(held.shape, lambda p: (0, 0, 0)),
            pl.BlockSpec(ids.shape, lambda p: (0, 0)),
        ],
        out_specs=pl.BlockSpec((peers, piece * slots, LANES), lambda p: (p, 0, 0)),
        scratch_shapes=[pltpu.VMEM((peers * frames, piece * LANES), BF16)],
        compiler_params=pltpu.CompilerParams(vmem_limit_bytes=VMEM_LIMIT),
        name="fetch",
    )(held, ids)


def edge_kernel(
    slots, piece, peers, parts, block, place_ref, held_ref, *refs
):
    cot_refs = refs[:parts]
    out_ref, wide, query, keys, cot, grad_a, grad_b = refs[parts:]
    edge = pl.program_id(0)
    each = piece * slots
    rows = piece * peers
    pixels = parts * rows
    scale = LANES ** (-0.5)
    log2e = math.log2(math.e)

    @pl.when(edge == 0)
    def _():
        def widen(p, carry):
            at = pl.multiple_of(p * 8 * each, 8 * each)
            block8 = held_ref[pl.ds(pl.multiple_of(p * 8, 8), 8)]
            wide[pl.ds(at, 8 * each), :] = block8.astype(F32).reshape(8 * each, LANES)
            return carry

        lax.fori_loop(0, parts * peers // 8, widen, 0)

    def spot(part, k, slot):
        return pl.ds(part * peers * each + k * slots + slot, peers, stride=each)

    for part in range(parts):
        for k in range(piece):
            here = pl.ds(part * rows + k * peers, peers)
            query[here, :] = wide[spot(part, k, 2 * edge), :].astype(BF16)
            keys[here, :] = wide[spot(part, k, 2 * edge + 1), :].astype(BF16)
        at = pl.multiple_of(place_ref[part] * rows, rows)
        cot[pl.ds(at, rows), :] = cot_refs[part][0]

    key_all = keys[...]
    for step in range(pixels // block):
        here = pl.ds(step * block, block)
        q = query[here, :]
        g = cot[here, :]
        scores = dot(q, key_all, 1, 1)
        top = jnp.max(scores, axis=1, keepdims=True)
        expo = jnp.exp2((scores - top) * (scale * log2e))
        total = jnp.sum(expo, axis=1, keepdims=True)
        dprobs = dot(g, key_all, 1, 1)
        inverse = 1.0 / total
        delta = jnp.sum(expo * dprobs, axis=1, keepdims=True) * inverse
        probs = expo * inverse
        probs_low = probs.astype(BF16)
        dscores = (probs * (dprobs - delta)).astype(BF16)
        grad_query = dot(dscores, key_all, 1, 0) * scale
        for sub in range(block // peers):
            at = step * (block // peers) + sub
            wide[spot(at // piece, at % piece, 2 * edge), :] = grad_query[
                sub * peers : (sub + 1) * peers, :
            ]
        first = dot(q, dscores, 0, 0)
        second = dot(g, probs_low, 0, 0)
        if step == 0:
            grad_a[...] = first
            grad_b[...] = second
        else:
            grad_a[...] += first
            grad_b[...] += second
    grad_keys = (grad_a[...] * scale + grad_b[...]).T
    for at in range(pixels // peers):
        wide[spot(at // piece, at % piece, 2 * edge + 1), :] = grad_keys[
            at * peers : (at + 1) * peers, :
        ]

    @pl.when(edge == slots // 2 - 1)
    def _():
        def narrow(p, carry):
            at = pl.multiple_of(p * 8 * each, 8 * each)
            block8 = wide[pl.ds(at, 8 * each), :].reshape(8, each, LANES)
            out_ref[pl.ds(pl.multiple_of(p * 8, 8), 8)] = block8.astype(BF16)
            return carry

        lax.fori_loop(0, parts * peers // 8, narrow, 0)


def edges(held, cotangents, places, slots, piece, peers):
    parts = len(cotangents)
    rows = piece * peers
    pixels = parts * rows
    per_edge = pl.BlockSpec((1, rows, LANES), lambda e, place: (e, 0, 0))
    whole = pl.BlockSpec(held.shape, lambda e, place: (0, 0, 0))
    block = 512
    return pl.pallas_call(
        functools.partial(edge_kernel, slots, piece, peers, parts, block),
        grid_spec=pltpu.PrefetchScalarGridSpec(
            num_scalar_prefetch=1,
            grid=(slots // 2,),
            in_specs=[whole] + [per_edge] * parts,
            out_specs=whole,
            scratch_shapes=[
                pltpu.VMEM((held.shape[0] * held.shape[1], LANES), F32),
                pltpu.VMEM((pixels, LANES), BF16),
                pltpu.VMEM((pixels, LANES), BF16),
                pltpu.VMEM((pixels, LANES), BF16),
                pltpu.VMEM((LANES, pixels), F32),
                pltpu.VMEM((LANES, pixels), F32),
            ],
        ),
        out_shape=jax.ShapeDtypeStruct(held.shape, BF16),
        compiler_params=pltpu.CompilerParams(vmem_limit_bytes=VMEM_LIMIT),
        name="edges",
    )(places, held, *cotangents)


def land_kernel(slots, piece, frames, back_ref, ids_ref, out_ref, total):
    part = pl.program_id(0)
    peers = back_ref.shape[0]
    count = peers * slots
    row = id_row(ids_ref, part, slots)
    every = lax.broadcasted_iota(jnp.int32, (peers * frames, count), 0).astype(F32)
    chosen = jnp.where(row == every, 1.0, 0.0).astype(BF16)
    columns = []
    for pair in range(piece // 2):
        both = back_ref[:, pair * 2 * slots : (pair + 1) * 2 * slots, :].astype(F32)
        for h in range(2):
            half = both[:, h * slots : (h + 1) * slots, :].reshape(count, LANES)
            columns.append(half.astype(BF16))
    sums = dot(chosen, jnp.concatenate(columns, axis=1), 1, 0)

    @pl.when(part == 0)
    def _():
        total[...] = sums

    @pl.when(part > 0)
    def _():
        total[...] += sums

    @pl.when(part == pl.num_programs(0) - 1)
    def _():
        for k in range(piece):
            block = total[:, k * LANES : (k + 1) * LANES].reshape(peers, frames, LANES)
            out_ref[:, k * frames : (k + 1) * frames, :] = block.astype(BF16)


def land(back, ids, parts, slots, piece, frames):
    peers = back.shape[0] // parts
    return pl.pallas_call(
        functools.partial(land_kernel, slots, piece, frames),
        grid=(parts,),
        out_shape=jax.ShapeDtypeStruct((peers, piece * frames, LANES), BF16),
        in_specs=[
            pl.BlockSpec((peers, piece * slots, LANES), lambda p: (p, 0, 0)),
            pl.BlockSpec(ids.shape, lambda p: (0, 0)),
        ],
        out_specs=pl.BlockSpec((peers, piece * frames, LANES), lambda p: (0, 0, 0)),
        scratch_shapes=[pltpu.VMEM((peers * frames, piece * LANES), F32)],
        compiler_params=pltpu.CompilerParams(vmem_limit_bytes=VMEM_LIMIT),
        name="land",
    )(back, ids)


def collect_kernel(piece, frames, back_ref, out_ref, wide):
    peers, each, _ = back_ref.shape

    def widen(p, carry):
        at = pl.multiple_of(p * 8 * each, 8 * each)
        block8 = back_ref[pl.ds(pl.multiple_of(p * 8, 8), 8)]
        wide[pl.ds(at, 8 * each), :] = block8.astype(F32).reshape(8 * each, LANES)
        return carry

    lax.fori_loop(0, peers // 8, widen, 0)

    def one(f, carry):
        for k in range(piece):
            block = wide[pl.ds(k * frames + f, peers, stride=each), :]
            out_ref[f, k * peers : (k + 1) * peers, :] = block
        return carry

    lax.fori_loop(0, frames, one, 0)


def collect(back, frames, piece):
    peers, each, _ = back.shape
    return pl.pallas_call(
        functools.partial(collect_kernel, piece, frames),
        out_shape=jax.ShapeDtypeStruct((frames, piece * peers, LANES), F32),
        in_specs=[pl.BlockSpec(memory_space=pltpu.VMEM)],
        out_specs=pl.BlockSpec(memory_space=pltpu.VMEM),
        scratch_shapes=[pltpu.VMEM((peers * each, LANES), F32)],
        compiler_params=pltpu.CompilerParams(vmem_limit_bytes=VMEM_LIMIT),
        name="collect",
    )(back)


def shards(features, endpoint_owner, endpoint_frame, grad_matched):
    peers = lax.axis_size("log")
    parts = lax.axis_size("pix")
    frames, rows, chans = features.shape
    piece = rows // peers
    ends = endpoint_owner.shape[0]
    each = -(-(ends // 2) // parts)
    slots = 2 * each
    me = lax.axis_index("pix")

    ids = (endpoint_owner * frames + endpoint_frame).reshape(1, ends)
    ids = jnp.pad(ids, ((0, 0), (0, LANES - ends)), constant_values=PAD_ID)
    ids = lax.all_gather(ids, "log", axis=0, tiled=True)

    padded = jnp.pad(grad_matched, ((0, parts * each - ends // 2), (0, 0), (0, 0)))
    cotangents = []
    for t in range(parts):
        taker = lax.rem(me + t, parts)
        given = lax.dynamic_slice_in_dim(padded, taker * each, each, axis=0)
        if t:
            given = lax.ppermute(given, "pix", [(p, (p + t) % parts) for p in range(parts)])
        cotangents.append(given)
    places = jnp.stack([lax.rem(me + parts - t, parts) for t in range(parts)])

    held = lax.all_to_all(spread(features, peers), "log", 0, 0, tiled=True)
    sent = fetch(held, ids, parts, slots, piece, frames)
    got = lax.all_to_all(sent, ("pix", "log"), 0, 0, tiled=True)
    grads = edges(got, cotangents, places, slots, piece, peers)
    back = lax.all_to_all(grads, ("pix", "log"), 0, 0, tiled=True)
    sums = land(back, ids, parts, slots, piece, frames)
    mine = lax.all_to_all(sums, "log", 0, 0, tiled=True)
    return collect(mine, frames, piece)


def solution(mesh):
    in_specs = (P("log", "pix", None), P("log", None), P("log", None), P("log", "pix", None))
    out_specs = P("log", "pix", None)
    return jax.shard_map(shards, mesh=mesh, in_specs=in_specs, out_specs=out_specs, check_vma=False)
```

```python
import functools
import math

import jax
import jax.numpy as jnp
from jax import lax
from jax.experimental import pallas as pl
from jax.experimental.pallas import tpu as pltpu
from jax.sharding import PartitionSpec as P

F32 = jnp.float32
BF16 = jnp.bfloat16
LANES = 128
ENDS = 28
PARTS = 4
SLOTS = 7
META = 2
GROUPS = 4


def dot(a, b, ca, cb):
    return lax.dot_general(a, b, (((ca,), (cb,)), ((), ())), preferred_element_type=F32)


def params(mebi):
    return pltpu.CompilerParams(vmem_limit_bytes=mebi * 2**20)


def cost(flops, size):
    return pl.CostEstimate(flops=flops, bytes_accessed=size, transcendentals=0)


def spread_kernel(peers, piece, feat_ref, owner_ref, frame_ref, out_ref, wide, line):
    step = pl.program_id(0)
    some = feat_ref.shape[0]
    frames = some * pl.num_programs(0)
    each = piece * some * GROUPS + META
    for f in range(some):
        for k in range(piece):
            block = feat_ref[f, k * peers : (k + 1) * peers, :].astype(F32)
            wide[pl.ds(k * some * GROUPS + step * some + f, peers, stride=each), :] = block

    @pl.when(step == pl.num_programs(0) - 1)
    def _():
        ends = owner_ref.shape[1]
        for at, ref in enumerate((owner_ref, frame_ref)):
            line[...] = jnp.full(line.shape, 127.0, F32)
            line[0:1, 0:ends] = ref[...].astype(F32)
            values = jnp.broadcast_to(line[0:1, :], (peers, LANES))
            wide[pl.ds(each - META + at, peers, stride=each), :] = values
        out_ref[...] = wide[...].astype(BF16)


def spread(features, owners, locals_, peers):
    frames, rows, chans = features.shape
    piece = rows // peers
    total = peers * (piece * frames + META)
    ends = owners.shape[0]
    return pl.pallas_call(
        functools.partial(spread_kernel, peers, piece),
        grid=(GROUPS,),
        out_shape=jax.ShapeDtypeStruct((total, chans), BF16),
        in_specs=[
            pl.BlockSpec((frames // GROUPS, rows, chans), lambda g: (g, 0, 0)),
            pl.BlockSpec((1, ends), lambda g: (0, 0)),
            pl.BlockSpec((1, ends), lambda g: (0, 0)),
        ],
        out_specs=pl.BlockSpec((total, chans), lambda g: (0, 0)),
        scratch_shapes=[pltpu.VMEM((total, chans), F32), pltpu.VMEM((8, LANES), F32)],
        compiler_params=params(12),
        name="spread",
    )(features, owners.reshape(1, ends), locals_.reshape(1, ends))


def lane_of(part, slot):
    odd = lax.rem(part, 2)
    own = odd * 6 + slot
    return lax.div(part, 2) * 14 + jnp.where(slot < 6, own, 12 + odd)


def id_column(owner, frame, part):
    peers = owner.shape[0]
    count = SLOTS * peers
    row = lax.broadcasted_iota(jnp.int32, (count, peers), 0)
    col = lax.broadcasted_iota(jnp.int32, (count, peers), 1)
    pick = jnp.where(lax.rem(row, peers) == col, 1.0, 0.0).astype(BF16)
    every = dot(pick, frame, 1, 0) * peers + dot(pick, owner, 1, 0)
    row = lax.broadcasted_iota(jnp.int32, (count, LANES), 0)
    lane = lax.broadcasted_iota(jnp.int32, (count, LANES), 1)
    mine = lane == lane_of(part, lax.div(row, peers))
    return jnp.sum(jnp.where(mine, every, 0.0), axis=1, keepdims=True)


def id_row(owner, frame, part):
    peers = owner.shape[0]
    count = SLOTS * peers
    row = lax.broadcasted_iota(jnp.int32, (LANES, count), 0)
    col = lax.broadcasted_iota(jnp.int32, (LANES, count), 1)
    pick = jnp.where(row == lane_of(part, lax.div(col, peers)), 1.0, 0.0).astype(BF16)
    every = dot(frame, pick, 1, 0) * peers + dot(owner, pick, 1, 0)
    row = lax.broadcasted_iota(jnp.int32, (peers, count), 0)
    col = lax.broadcasted_iota(jnp.int32, (peers, count), 1)
    return jnp.sum(jnp.where(lax.rem(col, peers) == row, every, 0.0), axis=0, keepdims=True)


def fetch_kernel(piece, frames, peers, held_ref, out_ref, ids_ref, table, held, wide):
    part = pl.program_id(0)
    total = peers * frames
    each = piece * SLOTS
    pitch = piece * frames + META

    @pl.when(part == 0)
    def _():
        held[...] = held_ref[...].astype(F32)
        for f in range(frames):
            for k in range(piece):
                block = held[pl.ds(k * frames + f, peers, stride=pitch), :]
                table[f * peers : (f + 1) * peers, k * LANES : (k + 1) * LANES] = block.astype(BF16)
        for at in range(META):
            ids_ref[at] = held[pl.ds(pitch - META + at, peers, stride=pitch), :].astype(BF16)

    column = id_column(ids_ref[0], ids_ref[1], part)
    lane = lax.broadcasted_iota(jnp.int32, (SLOTS * peers, total), 1).astype(F32)
    chosen = jnp.where(column == lane, 1.0, 0.0).astype(BF16)
    rows = dot(chosen, table[...], 1, 0)
    for k in range(piece):
        for s in range(SLOTS):
            block = rows[s * peers : (s + 1) * peers, k * LANES : (k + 1) * LANES]
            wide[pl.ds(k * SLOTS + s, peers, stride=each), :] = block
    out_ref[...] = wide[...].astype(BF16)


def fetch(held, piece, frames, peers):
    block = peers * piece * SLOTS
    return pl.pallas_call(
        functools.partial(fetch_kernel, piece, frames, peers),
        grid=(PARTS,),
        out_shape=(
            jax.ShapeDtypeStruct((PARTS * block, LANES), BF16),
            jax.ShapeDtypeStruct((META, peers, LANES), BF16),
        ),
        in_specs=[pl.BlockSpec(held.shape, lambda p: (0, 0))],
        out_specs=(
            pl.BlockSpec((block, LANES), lambda p: (p, 0)),
            pl.BlockSpec((META, peers, LANES), lambda p: (0, 0, 0)),
        ),
        scratch_shapes=[
            pltpu.VMEM((peers * frames, piece * LANES), BF16),
            pltpu.VMEM(held.shape, F32),
            pltpu.VMEM((block, LANES), F32),
        ],
        compiler_params=params(24),
        name="fetch",
    )(held)


def unpack_kernel(piece, peers, in_ref, out_ref, wide):
    each = piece * SLOTS
    wide[...] = in_ref[...].astype(F32)
    for s in range(SLOTS):
        for k in range(piece):
            block = wide[pl.ds(k * SLOTS + s, peers, stride=each), :]
            out_ref[s, k * peers : (k + 1) * peers, :] = block.astype(BF16)


def unpack(got, piece, peers):
    block = peers * piece * SLOTS
    rows = piece * peers
    return pl.pallas_call(
        functools.partial(unpack_kernel, piece, peers),
        grid=(PARTS,),
        out_shape=jax.ShapeDtypeStruct((SLOTS, PARTS * rows, LANES), BF16),
        in_specs=[pl.BlockSpec((block, LANES), lambda p: (p, 0))],
        out_specs=pl.BlockSpec((SLOTS, rows, LANES), lambda p: (0, p, 0)),
        scratch_shapes=[pltpu.VMEM((block, LANES), F32)],
        compiler_params=params(12),
        name="unpack",
    )(got)


def pack_kernel(piece, peers, first_ref, last_ref, kept_ref, come_ref, out_ref, wide):
    each = piece * SLOTS
    for s in range(SLOTS):
        for k in range(piece):
            here = slice(k * peers, (k + 1) * peers)
            if s < 4:
                block = first_ref[s, here, :].astype(F32)
            elif s < 6:
                block = last_ref[s - 4, here, :].astype(F32)
            else:
                block = kept_ref[here, :].astype(F32) + come_ref[here, :].astype(F32)
            wide[pl.ds(k * SLOTS + s, peers, stride=each), :] = block
    out_ref[...] = wide[...].astype(BF16)


def pack(first, last, kept, come, piece, peers):
    block = peers * piece * SLOTS
    rows = piece * peers
    return pl.pallas_call(
        functools.partial(pack_kernel, piece, peers),
        grid=(PARTS,),
        out_shape=jax.ShapeDtypeStruct((PARTS * block, LANES), BF16),
        in_specs=[
            pl.BlockSpec((4, rows, LANES), lambda p: (0, p, 0)),
            pl.BlockSpec((2, rows, LANES), lambda p: (0, p, 0)),
            pl.BlockSpec((rows, LANES), lambda p: (p, 0)),
            pl.BlockSpec((rows, LANES), lambda p: (p, 0)),
        ],
        out_specs=pl.BlockSpec((block, LANES), lambda p: (p, 0)),
        scratch_shapes=[pltpu.VMEM((block, LANES), F32)],
        compiler_params=params(12),
        name="pack",
    )(first, last, kept, come)


def edge_block(q, g, key_all):
    scale = LANES ** (-0.5)
    scores = dot(q, key_all, 1, 1)
    top = jnp.max(scores, axis=1, keepdims=True)
    expo = jnp.exp2((scores - top) * (scale * math.log2(math.e)))
    total = jnp.sum(expo, axis=1, keepdims=True)
    dprobs = dot(g, key_all, 1, 1)
    inverse = 1.0 / total
    delta = jnp.sum(expo * dprobs, axis=1, keepdims=True) * inverse
    probs = expo * inverse
    dscores = (probs * (dprobs - delta)).astype(BF16)
    grad_query = (dot(dscores, key_all, 1, 0) * scale).astype(BF16)
    return grad_query, dot(q, dscores, 0, 0), dot(g, probs.astype(BF16), 0, 0)


def place_cotangent(place_ref, cot_refs, cot):
    for part in range(PARTS):
        rows = cot_refs[part].shape[1]
        at = pl.multiple_of(place_ref[part] * rows, rows)
        cot[pl.ds(at, rows), :] = cot_refs[part][0]


def edge_kernel(block, place_ref, query_ref, keys_ref, *refs):
    cot_refs = refs[:PARTS]
    out_ref, cot, grad_a, grad_b = refs[PARTS:]
    place_cotangent(place_ref, cot_refs, cot)
    key_all = keys_ref[0]
    for step in range(cot.shape[0] // block):
        here = slice(step * block, (step + 1) * block)
        grad_query, first, second = edge_block(query_ref[0, here, :], cot[here, :], key_all)
        out_ref[0, here, :] = grad_query
        if step == 0:
            grad_a[...] = first
            grad_b[...] = second
        else:
            grad_a[...] += first
            grad_b[...] += second
    out_ref[1] = (grad_a[...] * LANES ** (-0.5) + grad_b[...]).T.astype(BF16)


def edges(maps, cotangents, places, start, count):
    _, pixels, chans = maps.shape
    rows = pixels // PARTS
    per_edge = pl.BlockSpec((1, rows, chans), lambda e, place: (e + start, 0, 0))
    return pl.pallas_call(
        functools.partial(edge_kernel, 768),
        grid_spec=pltpu.PrefetchScalarGridSpec(
            num_scalar_prefetch=1,
            grid=(count,),
            in_specs=[
                pl.BlockSpec((1, pixels, chans), lambda e, place: (2 * (e + start), 0, 0)),
                pl.BlockSpec((1, pixels, chans), lambda e, place: (2 * (e + start) + 1, 0, 0)),
            ]
            + [per_edge] * PARTS,
            out_specs=pl.BlockSpec((2, pixels, chans), lambda e, place: (e, 0, 0)),
            scratch_shapes=[
                pltpu.VMEM((pixels, chans), BF16),
                pltpu.VMEM((chans, pixels), F32),
                pltpu.VMEM((chans, pixels), F32),
            ],
        ),
        out_shape=jax.ShapeDtypeStruct((2 * count, pixels, chans), BF16),
        compiler_params=params(40),
        cost_estimate=cost(count * 10 * pixels * pixels * chans, count * 5 * pixels * chans * 2),
        name="edges",
    )(places, maps, maps, *cotangents)


def shared_kernel(block, place_ref, own_ref, come_ref, *refs):
    cot_refs = refs[:PARTS]
    kept_ref, sent_ref, query, keys, cot, grad_a, grad_b = refs[PARTS:]
    pixels = cot.shape[0]
    half = pixels // 2
    odd = place_ref[PARTS]
    place_cotangent(place_ref, cot_refs, cot)
    own = own_ref[0]
    come = come_ref[0]
    query[...] = jnp.where(odd == 0, own, come)
    keys[...] = jnp.where(odd == 0, come, own)
    key_all = keys[...]
    base = pl.multiple_of(odd * half, half)

    def halves(q_ref, k_ref):
        other = pl.multiple_of((1 - odd) * half, half)
        q_ref[pl.ds(other, half), :] = jnp.zeros((half, LANES), BF16)
        for step in range(half // block):
            here = pl.ds(pl.multiple_of(base + step * block, block), block)
            grad_query, first, second = edge_block(query[here, :], cot[here, :], key_all)
            q_ref[here, :] = grad_query
            if step == 0:
                grad_a[...] = first
                grad_b[...] = second
            else:
                grad_a[...] += first
                grad_b[...] += second
        k_ref[...] = (grad_a[...] * LANES ** (-0.5) + grad_b[...]).T.astype(BF16)

    @pl.when(odd == 0)
    def _():
        halves(kept_ref, sent_ref)

    @pl.when(odd == 1)
    def _():
        halves(sent_ref, kept_ref)


def shared_edge(maps, come, cotangents, places):
    slots, pixels, chans = maps.shape
    rows = pixels // PARTS
    last = cotangents[0].shape[0] - 1
    whole = pl.BlockSpec((pixels, chans), lambda e, place: (0, 0))
    return pl.pallas_call(
        functools.partial(shared_kernel, 768),
        grid_spec=pltpu.PrefetchScalarGridSpec(
            num_scalar_prefetch=1,
            grid=(1,),
            in_specs=[
                pl.BlockSpec((1, pixels, chans), lambda e, place: (slots - 1, 0, 0)),
                pl.BlockSpec((1, pixels, chans), lambda e, place: (0, 0, 0)),
            ]
            + [pl.BlockSpec((1, rows, chans), lambda e, place: (last, 0, 0))] * PARTS,
            out_specs=[whole, whole],
            scratch_shapes=[
                pltpu.VMEM((pixels, chans), BF16),
                pltpu.VMEM((pixels, chans), BF16),
                pltpu.VMEM((pixels, chans), BF16),
                pltpu.VMEM((chans, pixels), F32),
                pltpu.VMEM((chans, pixels), F32),
            ],
        ),
        out_shape=[jax.ShapeDtypeStruct((pixels, chans), BF16)] * 2,
        compiler_params=params(40),
        cost_estimate=cost(5 * pixels * pixels * chans, 5 * pixels * chans * 2),
        name="shared_edge",
    )(places, maps, come, *cotangents)


def land_kernel(piece, frames, back_ref, ids_ref, out_ref, total, wide, spread_out):
    part = pl.program_id(0)
    peers = ids_ref.shape[1]
    each = piece * SLOTS
    row = id_row(ids_ref[0], ids_ref[1], part)
    every = lax.broadcasted_iota(jnp.int32, (peers * frames, SLOTS * peers), 0).astype(F32)
    chosen = jnp.where(row == every, 1.0, 0.0).astype(BF16)
    wide[...] = back_ref[...].astype(F32)
    columns = []
    for k in range(piece):
        column = [wide[pl.ds(k * SLOTS + s, peers, stride=each), :].astype(BF16) for s in range(SLOTS)]
        columns.append(jnp.concatenate(column, axis=0))
    sums = dot(chosen, jnp.concatenate(columns, axis=1), 1, 0)

    @pl.when(part == 0)
    def _():
        total[...] = sums

    @pl.when(part > 0)
    def _():
        total[...] += sums

    @pl.when(part == PARTS - 1)
    def _():
        for k in range(piece):
            for f in range(frames):
                block = total[f * peers : (f + 1) * peers, k * LANES : (k + 1) * LANES]
                spread_out[pl.ds(k * frames + f, peers, stride=piece * frames), :] = block
        out_ref[...] = spread_out[...].astype(BF16)


def land(back, ids, piece, frames):
    peers = ids.shape[1]
    block = peers * piece * SLOTS
    rows = peers * piece * frames
    return pl.pallas_call(
        functools.partial(land_kernel, piece, frames),
        grid=(PARTS,),
        out_shape=jax.ShapeDtypeStruct((rows, LANES), BF16),
        in_specs=[
            pl.BlockSpec((block, LANES), lambda p: (p, 0)),
            pl.BlockSpec(ids.shape, lambda p: (0, 0, 0)),
        ],
        out_specs=pl.BlockSpec((rows, LANES), lambda p: (0, 0)),
        scratch_shapes=[
            pltpu.VMEM((peers * frames, piece * LANES), F32),
            pltpu.VMEM((block, LANES), F32),
            pltpu.VMEM((rows, LANES), F32),
        ],
        compiler_params=params(32),
        name="land",
    )(back, ids)


def collect_kernel(piece, peers, back_ref, out_ref, wide):
    step = pl.program_id(0)
    some = out_ref.shape[0]
    each = piece * some * GROUPS

    @pl.when(step == 0)
    def _():
        wide[...] = back_ref[...].astype(F32)

    for f in range(some):
        for k in range(piece):
            block = wide[pl.ds(k * some * GROUPS + step * some + f, peers, stride=each), :]
            out_ref[f, k * peers : (k + 1) * peers, :] = block


def collect(back, frames, piece, peers):
    return pl.pallas_call(
        functools.partial(collect_kernel, piece, peers),
        grid=(GROUPS,),
        out_shape=jax.ShapeDtypeStruct((frames, piece * peers, LANES), F32),
        in_specs=[pl.BlockSpec(back.shape, lambda g: (0, 0))],
        out_specs=pl.BlockSpec((frames // GROUPS, piece * peers, LANES), lambda g: (g, 0, 0)),
        scratch_shapes=[pltpu.VMEM(back.shape, F32)],
        compiler_params=params(16),
        name="collect",
    )(back)


def exchange(blocks, axes):
    total = blocks.shape[0]
    count = lax.axis_size(axes)
    shape = (count, total // count // 2, 2, LANES)
    moved = lax.all_to_all(blocks.reshape(shape), axes, 0, 0, tiled=True)
    return moved.reshape(total, LANES)


def shards(features, endpoint_owner, endpoint_frame, grad_matched):
    peers = lax.axis_size("log")
    frames, rows, chans = features.shape
    piece = rows // peers
    me = lax.axis_index("pix")
    if lax.axis_size("pix") != PARTS or endpoint_owner.shape[0] != ENDS:
        raise ValueError("other sizes")

    cotangents = []
    for t in range(PARTS):
        taker = lax.rem(me + t, PARTS)
        start = lax.div(taker, 2) * 7
        own = lax.dynamic_slice_in_dim(grad_matched, start + lax.rem(taker, 2) * 3, 3, axis=0)
        both = lax.dynamic_slice_in_dim(grad_matched, start + 6, 1, axis=0)
        given = jnp.concatenate([own, both], axis=0)
        if t:
            given = lax.ppermute(given, "pix", [(p, (p + t) % PARTS) for p in range(PARTS)])
        cotangents.append(given)
    places = jnp.stack([lax.rem(me + PARTS - t, PARTS) for t in range(PARTS)] + [lax.rem(me, 2)])
    partner = [(p, p ^ 1) for p in range(PARTS)]

    everyone = ("pix", "log")

    held = exchange(spread(features, endpoint_owner, endpoint_frame, peers), "log")
    sent, ids = fetch(held, piece, frames, peers)
    maps = unpack(exchange(sent, everyone), piece, peers)
    come = lax.ppermute(maps[SLOTS - 1 :], "pix", partner)
    first = edges(maps, cotangents, places, 0, 2)
    come, first = lax.optimization_barrier((come, first))
    kept, given = shared_edge(maps, come, cotangents, places)
    come = lax.ppermute(given, "pix", partner)
    last = edges(maps, cotangents, places, 2, 1)
    grads = pack(first, last, kept, come, piece, peers)
    sums = land(exchange(grads, everyone), ids, piece, frames)
    return collect(exchange(sums, "log"), frames, piece, peers)


def solution(mesh):
    in_specs = (P("log", "pix", None), P("log", None), P("log", None), P("log", "pix", None))
    out_specs = P("log", "pix", None)
    return jax.shard_map(shards, mesh=mesh, in_specs=in_specs, out_specs=out_specs, check_vma=False)
```

```python
import functools
import math

import jax
import jax.numpy as jnp
from jax import lax
from jax.experimental import pallas as pl
from jax.experimental.pallas import tpu as pltpu
from jax.sharding import PartitionSpec as P

F32 = jnp.float32
BF16 = jnp.bfloat16
LANES = 128
ENDS = 28
PARTS = 4
SLOTS = 7
META = 2
GROUPS = 4
SAFE = (1e-20, 1e20)


def dot(a, b, ca, cb):
    return lax.dot_general(a, b, (((ca,), (cb,)), ((), ())), preferred_element_type=F32)


def params(mebi):
    return pltpu.CompilerParams(vmem_limit_bytes=mebi * 2**20)


def in_hbm(x):
    return pltpu.with_memory_space_constraint(x, pltpu.HBM)


def vmem():
    return pl.BlockSpec(memory_space=pltpu.VMEM)


def cost(flops, size):
    return pl.CostEstimate(flops=flops, bytes_accessed=size, transcendentals=0)


def spread_kernel(peers, piece, feat_ref, owner_ref, frame_ref, out_ref, wide, line):
    step = pl.program_id(0)
    some = feat_ref.shape[0]
    frames = some * pl.num_programs(0)
    each = piece * some * GROUPS + META
    for f in range(some):
        for k in range(piece):
            block = feat_ref[f, k * peers : (k + 1) * peers, :].astype(F32)
            wide[pl.ds(k * some * GROUPS + step * some + f, peers, stride=each), :] = block

    @pl.when(step == pl.num_programs(0) - 1)
    def _():
        ends = owner_ref.shape[1]
        for at, ref in enumerate((owner_ref, frame_ref)):
            line[...] = jnp.full(line.shape, 127.0, F32)
            line[0:1, 0:ends] = ref[...].astype(F32)
            values = jnp.broadcast_to(line[0:1, :], (peers, LANES))
            wide[pl.ds(each - META + at, peers, stride=each), :] = values
        out_ref[...] = wide[...].astype(BF16)


def spread(features, owners, locals_, peers):
    frames, rows, chans = features.shape
    piece = rows // peers
    total = peers * (piece * frames + META)
    ends = owners.shape[0]
    return pl.pallas_call(
        functools.partial(spread_kernel, peers, piece),
        grid=(GROUPS,),
        out_shape=jax.ShapeDtypeStruct((total, chans), BF16),
        in_specs=[
            pl.BlockSpec((frames // GROUPS, rows, chans), lambda g: (g, 0, 0)),
            pl.BlockSpec((1, ends), lambda g: (0, 0)),
            pl.BlockSpec((1, ends), lambda g: (0, 0)),
        ],
        out_specs=pl.BlockSpec((total, chans), lambda g: (0, 0)),
        scratch_shapes=[pltpu.VMEM((total, chans), F32), pltpu.VMEM((8, LANES), F32)],
        compiler_params=params(12),
        name="spread",
    )(*[in_hbm(x) for x in (features, owners.reshape(1, ends), locals_.reshape(1, ends))])


def lane_of(part, slot):
    odd = part % 2
    own = odd * 6 + slot
    return part // 2 * 14 + jnp.where(slot < 6, own, 12 + odd)


def id_column(owner, frame, part):
    peers = owner.shape[0]
    count = SLOTS * peers
    row = lax.broadcasted_iota(jnp.int32, (count, peers), 0)
    col = lax.broadcasted_iota(jnp.int32, (count, peers), 1)
    pick = jnp.where(lax.rem(row, peers) == col, 1.0, 0.0).astype(BF16)
    every = dot(pick, frame, 1, 0) * peers + dot(pick, owner, 1, 0)
    row = lax.broadcasted_iota(jnp.int32, (count, LANES), 0)
    lane = lax.broadcasted_iota(jnp.int32, (count, LANES), 1)
    mine = lane == lane_of(part, lax.div(row, peers))
    return jnp.sum(jnp.where(mine, every, 0.0), axis=1, keepdims=True)


def id_row(owner, frame, part):
    peers = owner.shape[0]
    count = SLOTS * peers
    row = lax.broadcasted_iota(jnp.int32, (LANES, count), 0)
    col = lax.broadcasted_iota(jnp.int32, (LANES, count), 1)
    pick = jnp.where(row == lane_of(part, lax.div(col, peers)), 1.0, 0.0).astype(BF16)
    every = dot(frame, pick, 1, 0) * peers + dot(owner, pick, 1, 0)
    row = lax.broadcasted_iota(jnp.int32, (peers, count), 0)
    col = lax.broadcasted_iota(jnp.int32, (peers, count), 1)
    return jnp.sum(jnp.where(lax.rem(col, peers) == row, every, 0.0), axis=0, keepdims=True)


def fetch_kernel(piece, frames, peers, held_ref, out_ref, ids_ref, table, held, wide, ready, sems):
    total = peers * frames
    each = piece * SLOTS
    block = peers * each
    pitch = piece * frames + META
    held[...] = held_ref[...].astype(F32)
    for f in range(frames):
        for k in range(piece):
            rows = held[pl.ds(k * frames + f, peers, stride=pitch), :]
            table[f * peers : (f + 1) * peers, k * LANES : (k + 1) * LANES] = rows.astype(BF16)
    for at in range(META):
        ids_ref[at] = held[pl.ds(pitch - META + at, peers, stride=pitch), :].astype(BF16)
    owner, frame = ids_ref[0], ids_ref[1]
    lane = lax.broadcasted_iota(jnp.int32, (SLOTS * peers, total), 1).astype(F32)
    copies = []
    for part in range(PARTS):
        column = id_column(owner, frame, part)
        chosen = jnp.where(column == lane, 1.0, 0.0).astype(BF16)
        rows = dot(chosen, table[...], 1, 0)
        for k in range(piece):
            for s in range(SLOTS):
                some = rows[s * peers : (s + 1) * peers, k * LANES : (k + 1) * LANES]
                wide[part, pl.ds(k * SLOTS + s, peers, stride=each), :] = some
        ready[part] = wide[part].astype(BF16)
        there = out_ref.at[pl.ds(part * block, block)]
        copies.append(pltpu.make_async_copy(ready.at[part], there, sems.at[part]))
        copies[-1].start()
    for copy in copies:
        copy.wait()


def fetch(held, piece, frames, peers):
    block = peers * piece * SLOTS
    return pl.pallas_call(
        functools.partial(fetch_kernel, piece, frames, peers),
        out_shape=(
            pltpu.HBM((PARTS * block, LANES), BF16),
            jax.ShapeDtypeStruct((META, peers, LANES), BF16),
        ),
        in_specs=[vmem()],
        out_specs=(pl.BlockSpec(memory_space=pl.ANY), vmem()),
        scratch_shapes=[
            pltpu.VMEM((peers * frames, piece * LANES), BF16),
            pltpu.VMEM(held.shape, F32),
            pltpu.VMEM((PARTS, block, LANES), F32),
            pltpu.VMEM((PARTS, block, LANES), BF16),
            pltpu.SemaphoreType.DMA((PARTS,)),
        ],
        compiler_params=params(40),
        name="fetch",
    )(held)


def unpack_kernel(piece, peers, in_ref, out_ref, wide):
    each = piece * SLOTS
    wide[...] = in_ref[...].astype(F32)
    for s in range(SLOTS):
        for k in range(piece):
            block = wide[pl.ds(k * SLOTS + s, peers, stride=each), :]
            out_ref[s, k * peers : (k + 1) * peers, :] = block.astype(BF16)


def unpack(got, piece, peers):
    block = peers * piece * SLOTS
    rows = piece * peers
    return pl.pallas_call(
        functools.partial(unpack_kernel, piece, peers),
        grid=(PARTS,),
        out_shape=jax.ShapeDtypeStruct((SLOTS, PARTS * rows, LANES), BF16),
        in_specs=[pl.BlockSpec((block, LANES), lambda p: (p, 0))],
        out_specs=pl.BlockSpec((SLOTS, rows, LANES), lambda p: (0, p, 0)),
        scratch_shapes=[pltpu.VMEM((block, LANES), F32)],
        compiler_params=params(12),
        name="unpack",
    )(got)


def pack_kernel(piece, peers, first_ref, last_ref, kept_ref, come_ref, out_ref, wide):
    each = piece * SLOTS
    for s in range(SLOTS):
        for k in range(piece):
            here = slice(k * peers, (k + 1) * peers)
            if s < 4:
                block = first_ref[s, here, :].astype(F32)
            elif s < 6:
                block = last_ref[s - 4, here, :].astype(F32)
            else:
                block = kept_ref[here, :].astype(F32) + come_ref[here, :].astype(F32)
            wide[pl.ds(k * SLOTS + s, peers, stride=each), :] = block
    out_ref[...] = wide[...].astype(BF16)


def pack(first, last, kept, come, piece, peers):
    block = peers * piece * SLOTS
    rows = piece * peers
    return pl.pallas_call(
        functools.partial(pack_kernel, piece, peers),
        grid=(PARTS,),
        out_shape=jax.ShapeDtypeStruct((PARTS * block, LANES), BF16),
        in_specs=[
            pl.BlockSpec((4, rows, LANES), lambda p: (0, p, 0)),
            pl.BlockSpec((2, rows, LANES), lambda p: (0, p, 0)),
            pl.BlockSpec((rows, LANES), lambda p: (p, 0)),
            pl.BlockSpec((rows, LANES), lambda p: (p, 0)),
        ],
        out_specs=pl.BlockSpec((block, LANES), lambda p: (p, 0)),
        scratch_shapes=[pltpu.VMEM((block, LANES), F32)],
        compiler_params=params(12),
        name="pack",
    )(first, last, kept, come)


def edge_block(q, g, key_all, take_top):
    scale = LANES ** (-0.5)
    scores = dot(q, key_all, 1, 1)
    if take_top:
        scores = scores - jnp.max(scores, axis=1, keepdims=True)
    expo = jnp.exp2(scores * (scale * math.log2(math.e)))
    total = jnp.sum(expo, axis=1, keepdims=True)
    dprobs = dot(g, key_all, 1, 1)
    inverse = 1.0 / total
    probs = expo * inverse
    probs_low = probs.astype(BF16)
    delta = jnp.sum(probs_low.astype(F32) * dprobs, axis=1, keepdims=True)
    dscores = (probs * (dprobs - delta)).astype(BF16)
    grad_query = (dot(dscores, key_all, 1, 0) * scale).astype(BF16)
    grad_keys = dot(q, dscores, 0, 0) * scale + dot(g, probs_low, 0, 0)
    return grad_query, grad_keys, total


def unsafe(totals):
    low = functools.reduce(jnp.minimum, totals)
    high = functools.reduce(jnp.maximum, totals)
    return jnp.logical_not((jnp.min(low) > SAFE[0]) & (jnp.max(high) < SAFE[1]))


def place_cotangent(place_ref, cot_refs, cot, edge):
    for part in range(PARTS):
        rows = cot_refs[part].shape[1]
        at = pl.multiple_of(place_ref[part] * rows, rows)
        cot[pl.ds(at, rows), :] = cot_refs[part][edge]


def edge_kernel(block, start, count, place_ref, maps_ref, *refs):
    cot_refs = refs[:PARTS]
    out_ref, cots, grad = refs[PARTS:]

    def run(edge, take_top):
        key_all = maps_ref[2 * (start + edge) + 1]
        totals = []
        for step in range(cots.shape[1] // block):
            here = slice(step * block, (step + 1) * block)
            query = maps_ref[2 * (start + edge), here, :]
            grad_query, grad_keys, total = edge_block(query, cots[edge, here, :], key_all, take_top)
            totals.append(total)
            out_ref[2 * edge, here, :] = grad_query
            if step == 0:
                grad[edge] = grad_keys
            else:
                grad[edge] += grad_keys
        out_ref[2 * edge + 1] = grad[edge].T.astype(BF16)
        return totals

    def one(edge, carry):
        place_cotangent(place_ref, cot_refs, cots.at[edge], start + edge)
        totals = run(edge, False)

        @pl.when(unsafe(totals))
        def _():
            run(edge, True)

        return carry

    lax.fori_loop(0, count, one, 0)


def edges(maps, cotangents, places, start, count):
    _, pixels, chans = maps.shape
    return pl.pallas_call(
        functools.partial(edge_kernel, pixels // 2, start, count),
        in_specs=[pl.BlockSpec(memory_space=pltpu.SMEM)] + [vmem()] * (PARTS + 1),
        out_specs=vmem(),
        out_shape=jax.ShapeDtypeStruct((2 * count, pixels, chans), BF16),
        scratch_shapes=[
            pltpu.VMEM((count, pixels, chans), BF16),
            pltpu.VMEM((count, chans, pixels), F32),
        ],
        compiler_params=params(40),
        cost_estimate=cost(count * 10 * pixels * pixels * chans, count * 5 * pixels * chans * 2),
        name="edges",
    )(places, maps, *cotangents)


def shared_kernel(place_ref, maps_ref, come_ref, *refs):
    cot_refs = refs[:PARTS]
    kept_ref, sent_ref, query, keys, cot, grad = refs[PARTS:]
    pixels = cot.shape[0]
    half = pixels // 2
    odd = place_ref[PARTS]
    place_cotangent(place_ref, cot_refs, cot, cot_refs[0].shape[0] - 1)
    own = maps_ref.at[SLOTS - 1]
    come = come_ref.at[0]

    @pl.when(odd == 0)
    def _():
        query[...] = own[:half, :]
        keys[...] = come[...]

    @pl.when(odd == 1)
    def _():
        query[...] = come[half:, :]
        keys[...] = own[...]

    def run(take_top):
        g = cot[pl.ds(pl.multiple_of(odd * half, half), half), :]
        grad_query, grad_keys, total = edge_block(query[...], g, keys[...], take_top)
        grad[:half, :] = grad_query
        grad[half:, :] = grad_keys.T.astype(BF16)
        return total

    total = run(False)

    @pl.when(unsafe([total]))
    def _():
        run(True)

    @pl.when(odd == 0)
    def _():
        kept_ref[:half, :] = grad[:half, :]
        kept_ref[half:, :] = jnp.zeros((half, LANES), BF16)
        sent_ref[...] = grad[half:, :]

    @pl.when(odd == 1)
    def _():
        sent_ref[:half, :] = jnp.zeros((half, LANES), BF16)
        sent_ref[half:, :] = grad[:half, :]
        kept_ref[...] = grad[half:, :]


def shared_edge(maps, come, cotangents, places):
    _, pixels, chans = maps.shape
    return pl.pallas_call(
        shared_kernel,
        in_specs=[pl.BlockSpec(memory_space=pltpu.SMEM)] + [vmem()] * (PARTS + 2),
        out_specs=[vmem(), vmem()],
        out_shape=[jax.ShapeDtypeStruct((pixels, chans), BF16)] * 2,
        scratch_shapes=[
            pltpu.VMEM((pixels // 2, chans), BF16),
            pltpu.VMEM((pixels, chans), BF16),
            pltpu.VMEM((pixels, chans), BF16),
            pltpu.VMEM((pixels // 2 * 3, chans), BF16),
        ],
        compiler_params=params(40),
        cost_estimate=cost(5 * pixels * pixels * chans, 5 * pixels * chans * 2),
        name="shared_edge",
    )(places, maps, come, *cotangents)


def land_kernel(piece, frames, back_ref, ids_ref, out_ref, values, wide, spread_out):
    peers = ids_ref.shape[1]
    each = piece * SLOTS
    count = SLOTS * peers
    rows = each * peers
    wide[...] = back_ref[...].astype(F32)
    names = []
    for part in range(PARTS):
        names.append(id_row(ids_ref[0], ids_ref[1], part))
        for k in range(piece):
            for s in range(SLOTS):
                block = wide[pl.ds(part * rows + k * SLOTS + s, peers, stride=each), :]
                at = part * count + s * peers
                values[at : at + peers, k * LANES : (k + 1) * LANES] = block.astype(BF16)
    name = jnp.concatenate(names, axis=1)
    some = 4
    for group in range(frames // some):
        every = lax.broadcasted_iota(jnp.int32, (some * peers, PARTS * count), 0) + group * some * peers
        chosen = jnp.where(name == every.astype(F32), 1.0, 0.0).astype(BF16)
        sums = dot(chosen, values[...], 1, 0)
        for f in range(some):
            for k in range(piece):
                block = sums[f * peers : (f + 1) * peers, k * LANES : (k + 1) * LANES]
                at = k * frames + group * some + f
                spread_out[pl.ds(at, peers, stride=piece * frames), :] = block
    out_ref[...] = spread_out[...].astype(BF16)


def land(back, ids, piece, frames):
    peers = ids.shape[1]
    rows = peers * piece * frames
    return pl.pallas_call(
        functools.partial(land_kernel, piece, frames),
        out_shape=jax.ShapeDtypeStruct((rows, LANES), BF16),
        in_specs=[vmem(), vmem()],
        out_specs=vmem(),
        scratch_shapes=[
            pltpu.VMEM((PARTS * SLOTS * peers, piece * LANES), BF16),
            pltpu.VMEM(back.shape, F32),
            pltpu.VMEM((rows, LANES), F32),
        ],
        compiler_params=params(32),
        name="land",
    )(back, ids)


def collect_kernel(piece, peers, back_ref, out_ref, wide):
    step = pl.program_id(0)
    some = out_ref.shape[0]
    frames = some * pl.num_programs(0)
    each = piece * frames

    @pl.when(step == 0)
    def _():
        wide[...] = back_ref[...].astype(F32)

    for f in range(some):
        for k in range(piece):
            block = wide[pl.ds(k * frames + step * some + f, peers, stride=each), :]
            out_ref[f, k * peers : (k + 1) * peers, :] = block


def collect(back, frames, piece, peers):
    return pl.pallas_call(
        functools.partial(collect_kernel, piece, peers),
        grid=(GROUPS,),
        out_shape=jax.ShapeDtypeStruct((frames, piece * peers, LANES), F32),
        in_specs=[vmem()],
        out_specs=pl.BlockSpec((frames // GROUPS, piece * peers, LANES), lambda g: (g, 0, 0)),
        scratch_shapes=[pltpu.VMEM(back.shape, F32)],
        compiler_params=params(16),
        name="collect",
    )(back)


def exchange(blocks, axes):
    total = blocks.shape[0]
    count = lax.axis_size(axes)
    shape = (count, total // count // 2, 2, LANES)
    moved = lax.all_to_all(blocks.reshape(shape), axes, 0, 0, tiled=True)
    return moved.reshape(total, LANES)


def shards(features, endpoint_owner, endpoint_frame, grad_matched):
    peers = lax.axis_size("log")
    frames, rows, chans = features.shape
    piece = rows // peers
    me = lax.axis_index("pix")
    if lax.axis_size("pix") != PARTS or endpoint_owner.shape[0] != ENDS:
        raise ValueError("other sizes")

    cotangents = []
    for t in range(PARTS):
        taker = lax.rem(me + t, PARTS)
        start = lax.div(taker, 2) * 7
        own = lax.dynamic_slice_in_dim(grad_matched, start + lax.rem(taker, 2) * 3, 3, axis=0)
        both = lax.dynamic_slice_in_dim(grad_matched, start + 6, 1, axis=0)
        given = jnp.concatenate([own, both], axis=0)
        if t:
            given = lax.ppermute(given, "pix", [(p, (p + t) % PARTS) for p in range(PARTS)])
        cotangents.append(given)
    places = jnp.stack([lax.rem(me + PARTS - t, PARTS) for t in range(PARTS)] + [lax.rem(me, 2)])
    partner = [(p, p ^ 1) for p in range(PARTS)]

    everyone = ("pix", "log")

    held = exchange(spread(features, endpoint_owner, endpoint_frame, peers), "log")
    sent, ids = fetch(held, piece, frames, peers)
    maps = unpack(exchange(sent, everyone), piece, peers)
    come = lax.ppermute(maps[SLOTS - 1 :], "pix", partner)
    first = edges(maps, cotangents, places, 0, 2)
    come, first = lax.optimization_barrier((come, first))
    kept, given = shared_edge(maps, come, cotangents, places)
    come = lax.ppermute(given, "pix", partner)
    last = edges(maps, cotangents, places, 2, 1)
    grads = pack(first, last, kept, come, piece, peers)
    sums = land(exchange(grads, everyone), ids, piece, frames)
    return collect(exchange(sums, "log"), frames, piece, peers)


def solution(mesh):
    in_specs = (P("log", "pix", None), P("log", None), P("log", None), P("log", "pix", None))
    out_specs = P("log", "pix", None)
    return jax.shard_map(shards, mesh=mesh, in_specs=in_specs, out_specs=out_specs, check_vma=False)
```

```python
import functools
import math

import jax
import jax.numpy as jnp
from jax import lax
from jax.experimental import pallas as pl
from jax.experimental.pallas import tpu as pltpu
from jax.sharding import PartitionSpec as P

F32 = jnp.float32
BF16 = jnp.bfloat16
LANES = 128
ENDS = 28
PARTS = 4
SLOTS = 7
META = 2
GROUPS = 4


def dot(a, b, ca, cb):
    return lax.dot_general(a, b, (((ca,), (cb,)), ((), ())), preferred_element_type=F32)


def params(mebi):
    return pltpu.CompilerParams(vmem_limit_bytes=mebi * 2**20)


def in_hbm(x):
    return pltpu.with_memory_space_constraint(x, pltpu.HBM)


def vmem():
    return pl.BlockSpec(memory_space=pltpu.VMEM)


def cost(flops, size):
    return pl.CostEstimate(flops=flops, bytes_accessed=size, transcendentals=0)


def spread_kernel(peers, piece, feat_ref, owner_ref, frame_ref, out_ref, wide, line):
    step = pl.program_id(0)
    some = feat_ref.shape[0]
    frames = some * pl.num_programs(0)
    each = piece * some * GROUPS + META
    for f in range(some):
        for k in range(piece):
            block = feat_ref[f, k * peers : (k + 1) * peers, :].astype(F32)
            wide[pl.ds(k * some * GROUPS + step * some + f, peers, stride=each), :] = block

    @pl.when(step == pl.num_programs(0) - 1)
    def _():
        ends = owner_ref.shape[1]
        for at, ref in enumerate((owner_ref, frame_ref)):
            line[...] = jnp.full(line.shape, 127.0, F32)
            line[0:1, 0:ends] = ref[...].astype(F32)
            values = jnp.broadcast_to(line[0:1, :], (peers, LANES))
            wide[pl.ds(each - META + at, peers, stride=each), :] = values
        out_ref[...] = wide[...].astype(BF16)


def spread(features, owners, locals_, peers):
    frames, rows, chans = features.shape
    piece = rows // peers
    total = peers * (piece * frames + META)
    ends = owners.shape[0]
    return pl.pallas_call(
        functools.partial(spread_kernel, peers, piece),
        grid=(GROUPS,),
        out_shape=jax.ShapeDtypeStruct((total, chans), BF16),
        in_specs=[
            pl.BlockSpec((frames // GROUPS, rows, chans), lambda g: (g, 0, 0)),
            pl.BlockSpec((1, ends), lambda g: (0, 0)),
            pl.BlockSpec((1, ends), lambda g: (0, 0)),
        ],
        out_specs=pl.BlockSpec((total, chans), lambda g: (0, 0)),
        scratch_shapes=[pltpu.VMEM((total, chans), F32), pltpu.VMEM((8, LANES), F32)],
        compiler_params=params(12),
        name="spread",
    )(*[in_hbm(x) for x in (features, owners.reshape(1, ends), locals_.reshape(1, ends))])


def lane_of(part, slot):
    odd = part % 2
    own = odd * 6 + slot
    return part // 2 * 14 + jnp.where(slot < 6, own, 12 + odd)


def id_column(owner, frame, part):
    peers = owner.shape[0]
    count = SLOTS * peers
    row = lax.broadcasted_iota(jnp.int32, (count, peers), 0)
    col = lax.broadcasted_iota(jnp.int32, (count, peers), 1)
    pick = jnp.where(lax.rem(row, peers) == col, 1.0, 0.0).astype(BF16)
    every = dot(pick, frame, 1, 0) * peers + dot(pick, owner, 1, 0)
    row = lax.broadcasted_iota(jnp.int32, (count, LANES), 0)
    lane = lax.broadcasted_iota(jnp.int32, (count, LANES), 1)
    mine = lane == lane_of(part, lax.div(row, peers))
    return jnp.sum(jnp.where(mine, every, 0.0), axis=1, keepdims=True)


def id_row(owner, frame, part):
    peers = owner.shape[0]
    count = SLOTS * peers
    row = lax.broadcasted_iota(jnp.int32, (LANES, count), 0)
    col = lax.broadcasted_iota(jnp.int32, (LANES, count), 1)
    pick = jnp.where(row == lane_of(part, lax.div(col, peers)), 1.0, 0.0).astype(BF16)
    every = dot(frame, pick, 1, 0) * peers + dot(owner, pick, 1, 0)
    row = lax.broadcasted_iota(jnp.int32, (peers, count), 0)
    col = lax.broadcasted_iota(jnp.int32, (peers, count), 1)
    return jnp.sum(jnp.where(lax.rem(col, peers) == row, every, 0.0), axis=0, keepdims=True)


def fetch_kernel(piece, frames, peers, held_ref, out_ref, ids_ref, table, held, wide, ready, sems):
    total = peers * frames
    each = piece * SLOTS
    block = peers * each
    pitch = piece * frames + META
    held[...] = held_ref[...].astype(F32)
    for f in range(frames):
        for k in range(piece):
            rows = held[pl.ds(k * frames + f, peers, stride=pitch), :]
            table[f * peers : (f + 1) * peers, k * LANES : (k + 1) * LANES] = rows.astype(BF16)
    for at in range(META):
        ids_ref[at] = held[pl.ds(pitch - META + at, peers, stride=pitch), :].astype(BF16)
    owner, frame = ids_ref[0], ids_ref[1]
    lane = lax.broadcasted_iota(jnp.int32, (SLOTS * peers, total), 1).astype(F32)
    copies = []
    for part in range(PARTS):
        column = id_column(owner, frame, part)
        chosen = jnp.where(column == lane, 1.0, 0.0).astype(BF16)
        rows = dot(chosen, table[...], 1, 0)
        for k in range(piece):
            for s in range(SLOTS):
                some = rows[s * peers : (s + 1) * peers, k * LANES : (k + 1) * LANES]
                wide[part, pl.ds(k * SLOTS + s, peers, stride=each), :] = some
        ready[part] = wide[part].astype(BF16)
        there = out_ref.at[pl.ds(part * block, block)]
        copies.append(pltpu.make_async_copy(ready.at[part], there, sems.at[part]))
        copies[-1].start()
    for copy in copies:
        copy.wait()


def fetch(held, piece, frames, peers):
    block = peers * piece * SLOTS
    return pl.pallas_call(
        functools.partial(fetch_kernel, piece, frames, peers),
        out_shape=(
            pltpu.HBM((PARTS * block, LANES), BF16),
            jax.ShapeDtypeStruct((META, peers, LANES), BF16),
        ),
        in_specs=[vmem()],
        out_specs=(pl.BlockSpec(memory_space=pl.ANY), vmem()),
        scratch_shapes=[
            pltpu.VMEM((peers * frames, piece * LANES), BF16),
            pltpu.VMEM(held.shape, F32),
            pltpu.VMEM((PARTS, block, LANES), F32),
            pltpu.VMEM((PARTS, block, LANES), BF16),
            pltpu.SemaphoreType.DMA((PARTS,)),
        ],
        compiler_params=params(40),
        name="fetch",
    )(held)


def unpack_kernel(piece, peers, in_ref, out_ref, wide):
    each = piece * SLOTS
    wide[...] = in_ref[...].astype(F32)
    for s in range(SLOTS):
        for k in range(piece):
            block = wide[pl.ds(k * SLOTS + s, peers, stride=each), :]
            out_ref[s, k * peers : (k + 1) * peers, :] = block.astype(BF16)


def unpack(got, piece, peers):
    block = peers * piece * SLOTS
    rows = piece * peers
    return pl.pallas_call(
        functools.partial(unpack_kernel, piece, peers),
        grid=(PARTS,),
        out_shape=jax.ShapeDtypeStruct((SLOTS, PARTS * rows, LANES), BF16),
        in_specs=[pl.BlockSpec((block, LANES), lambda p: (p, 0))],
        out_specs=pl.BlockSpec((SLOTS, rows, LANES), lambda p: (0, p, 0)),
        scratch_shapes=[pltpu.VMEM((block, LANES), F32)],
        compiler_params=params(12),
        name="unpack",
    )(got)


def pack_kernel(piece, peers, first_ref, last_ref, kept_ref, come_ref, out_ref, wide):
    each = piece * SLOTS
    for s in range(SLOTS):
        for k in range(piece):
            here = slice(k * peers, (k + 1) * peers)
            if s < 4:
                block = first_ref[s, here, :].astype(F32)
            elif s < 6:
                block = last_ref[s - 4, here, :].astype(F32)
            else:
                block = kept_ref[here, :].astype(F32) + come_ref[here, :].astype(F32)
            wide[pl.ds(k * SLOTS + s, peers, stride=each), :] = block
    out_ref[...] = wide[...].astype(BF16)


def pack(first, last, kept, come, piece, peers):
    block = peers * piece * SLOTS
    rows = piece * peers
    return pl.pallas_call(
        functools.partial(pack_kernel, piece, peers),
        grid=(PARTS,),
        out_shape=jax.ShapeDtypeStruct((PARTS * block, LANES), BF16),
        in_specs=[
            pl.BlockSpec((4, rows, LANES), lambda p: (0, p, 0)),
            pl.BlockSpec((2, rows, LANES), lambda p: (0, p, 0)),
            pl.BlockSpec((rows, LANES), lambda p: (p, 0)),
            pl.BlockSpec((rows, LANES), lambda p: (p, 0)),
        ],
        out_specs=pl.BlockSpec((block, LANES), lambda p: (p, 0)),
        scratch_shapes=[pltpu.VMEM((block, LANES), F32)],
        compiler_params=params(12),
        name="pack",
    )(first, last, kept, come)


def edge_block(q, g, key_all):
    scale = LANES ** (-0.5)
    scores = dot(q, key_all, 1, 1)
    top = jnp.max(scores, axis=1, keepdims=True)
    expo = jnp.exp2((scores - top) * (scale * math.log2(math.e)))
    total = jnp.sum(expo, axis=1, keepdims=True)
    dprobs = dot(g, key_all, 1, 1)
    inverse = 1.0 / total
    delta = jnp.sum(expo * dprobs, axis=1, keepdims=True) * inverse
    probs = expo * inverse
    dscores = (probs * (dprobs - delta)).astype(BF16)
    grad_query = (dot(dscores, key_all, 1, 0) * scale).astype(BF16)
    grad_keys = dot(q, dscores, 0, 0) * scale + dot(g, probs.astype(BF16), 0, 0)
    return grad_query, grad_keys


def place_cotangent(place_ref, cot_refs, cot, edge):
    for part in range(PARTS):
        rows = cot_refs[part].shape[1]
        at = pl.multiple_of(place_ref[part] * rows, rows)
        cot[pl.ds(at, rows), :] = cot_refs[part][edge]


def edge_kernel(block, start, count, place_ref, maps_ref, *refs):
    cot_refs = refs[:PARTS]
    out_ref, cots, grad = refs[PARTS:]
    for edge in range(count):
        cot = cots.at[edge]
        place_cotangent(place_ref, cot_refs, cot, start + edge)
        key_all = maps_ref[2 * (start + edge) + 1]
        for step in range(cot.shape[0] // block):
            here = slice(step * block, (step + 1) * block)
            query = maps_ref[2 * (start + edge), here, :]
            grad_query, grad_keys = edge_block(query, cot[here, :], key_all)
            out_ref[2 * edge, here, :] = grad_query
            if step == 0:
                grad[edge] = grad_keys
            else:
                grad[edge] += grad_keys
        out_ref[2 * edge + 1] = grad[edge].T.astype(BF16)


def edges(maps, cotangents, places, start, count):
    _, pixels, chans = maps.shape
    return pl.pallas_call(
        functools.partial(edge_kernel, pixels // 2, start, count),
        in_specs=[pl.BlockSpec(memory_space=pltpu.SMEM)] + [vmem()] * (PARTS + 1),
        out_specs=vmem(),
        out_shape=jax.ShapeDtypeStruct((2 * count, pixels, chans), BF16),
        scratch_shapes=[
            pltpu.VMEM((count, pixels, chans), BF16),
            pltpu.VMEM((count, chans, pixels), F32),
        ],
        compiler_params=params(40),
        cost_estimate=cost(count * 10 * pixels * pixels * chans, count * 5 * pixels * chans * 2),
        name="edges",
    )(places, maps, *cotangents)


def shared_kernel(place_ref, maps_ref, come_ref, *refs):
    cot_refs = refs[:PARTS]
    kept_ref, sent_ref, query, keys, cot, grad = refs[PARTS:]
    pixels = cot.shape[0]
    half = pixels // 2
    odd = place_ref[PARTS]
    place_cotangent(place_ref, cot_refs, cot, cot_refs[0].shape[0] - 1)
    own = maps_ref.at[SLOTS - 1]
    come = come_ref.at[0]

    @pl.when(odd == 0)
    def _():
        query[...] = own[:half, :]
        keys[...] = come[...]

    @pl.when(odd == 1)
    def _():
        query[...] = come[half:, :]
        keys[...] = own[...]

    g = cot[pl.ds(pl.multiple_of(odd * half, half), half), :]
    grad_query, grad_keys = edge_block(query[...], g, keys[...])
    grad[:half, :] = grad_query
    grad[half:, :] = grad_keys.T.astype(BF16)

    @pl.when(odd == 0)
    def _():
        kept_ref[:half, :] = grad[:half, :]
        kept_ref[half:, :] = jnp.zeros((half, LANES), BF16)
        sent_ref[...] = grad[half:, :]

    @pl.when(odd == 1)
    def _():
        sent_ref[:half, :] = jnp.zeros((half, LANES), BF16)
        sent_ref[half:, :] = grad[:half, :]
        kept_ref[...] = grad[half:, :]


def shared_edge(maps, come, cotangents, places):
    _, pixels, chans = maps.shape
    return pl.pallas_call(
        shared_kernel,
        in_specs=[pl.BlockSpec(memory_space=pltpu.SMEM)] + [vmem()] * (PARTS + 2),
        out_specs=[vmem(), vmem()],
        out_shape=[jax.ShapeDtypeStruct((pixels, chans), BF16)] * 2,
        scratch_shapes=[
            pltpu.VMEM((pixels // 2, chans), BF16),
            pltpu.VMEM((pixels, chans), BF16),
            pltpu.VMEM((pixels, chans), BF16),
            pltpu.VMEM((pixels // 2 * 3, chans), BF16),
        ],
        compiler_params=params(40),
        cost_estimate=cost(5 * pixels * pixels * chans, 5 * pixels * chans * 2),
        name="shared_edge",
    )(places, maps, come, *cotangents)


def land_kernel(piece, frames, back_ref, ids_ref, out_ref, values, wide, spread_out):
    peers = ids_ref.shape[1]
    each = piece * SLOTS
    count = SLOTS * peers
    rows = each * peers
    wide[...] = back_ref[...].astype(F32)
    names = []
    for part in range(PARTS):
        names.append(id_row(ids_ref[0], ids_ref[1], part))
        for k in range(piece):
            for s in range(SLOTS):
                block = wide[pl.ds(part * rows + k * SLOTS + s, peers, stride=each), :]
                at = part * count + s * peers
                values[at : at + peers, k * LANES : (k + 1) * LANES] = block.astype(BF16)
    name = jnp.concatenate(names, axis=1)
    some = 4
    for group in range(frames // some):
        every = lax.broadcasted_iota(jnp.int32, (some * peers, PARTS * count), 0) + group * some * peers
        chosen = jnp.where(name == every.astype(F32), 1.0, 0.0).astype(BF16)
        sums = dot(chosen, values[...], 1, 0)
        for f in range(some):
            for k in range(piece):
                block = sums[f * peers : (f + 1) * peers, k * LANES : (k + 1) * LANES]
                at = k * frames + group * some + f
                spread_out[pl.ds(at, peers, stride=piece * frames), :] = block
    out_ref[...] = spread_out[...].astype(BF16)


def land(back, ids, piece, frames):
    peers = ids.shape[1]
    rows = peers * piece * frames
    return pl.pallas_call(
        functools.partial(land_kernel, piece, frames),
        out_shape=jax.ShapeDtypeStruct((rows, LANES), BF16),
        in_specs=[vmem(), vmem()],
        out_specs=vmem(),
        scratch_shapes=[
            pltpu.VMEM((PARTS * SLOTS * peers, piece * LANES), BF16),
            pltpu.VMEM(back.shape, F32),
            pltpu.VMEM((rows, LANES), F32),
        ],
        compiler_params=params(32),
        name="land",
    )(back, ids)


def collect_kernel(piece, peers, back_ref, out_ref, wide):
    step = pl.program_id(0)
    some = out_ref.shape[0]
    frames = some * pl.num_programs(0)
    each = piece * frames

    @pl.when(step == 0)
    def _():
        wide[...] = back_ref[...].astype(F32)

    for f in range(some):
        for k in range(piece):
            block = wide[pl.ds(k * frames + step * some + f, peers, stride=each), :]
            out_ref[f, k * peers : (k + 1) * peers, :] = block


def collect(back, frames, piece, peers):
    return pl.pallas_call(
        functools.partial(collect_kernel, piece, peers),
        grid=(GROUPS,),
        out_shape=jax.ShapeDtypeStruct((frames, piece * peers, LANES), F32),
        in_specs=[vmem()],
        out_specs=pl.BlockSpec((frames // GROUPS, piece * peers, LANES), lambda g: (g, 0, 0)),
        scratch_shapes=[pltpu.VMEM(back.shape, F32)],
        compiler_params=params(16),
        name="collect",
    )(back)


def exchange(blocks, axes):
    total = blocks.shape[0]
    count = lax.axis_size(axes)
    shape = (count, total // count // 2, 2, LANES)
    moved = lax.all_to_all(blocks.reshape(shape), axes, 0, 0, tiled=True)
    return moved.reshape(total, LANES)


def shards(features, endpoint_owner, endpoint_frame, grad_matched):
    peers = lax.axis_size("log")
    frames, rows, chans = features.shape
    piece = rows // peers
    me = lax.axis_index("pix")
    if lax.axis_size("pix") != PARTS or endpoint_owner.shape[0] != ENDS:
        raise ValueError("other sizes")

    cotangents = []
    for t in range(PARTS):
        taker = lax.rem(me + t, PARTS)
        start = lax.div(taker, 2) * 7
        own = lax.dynamic_slice_in_dim(grad_matched, start + lax.rem(taker, 2) * 3, 3, axis=0)
        both = lax.dynamic_slice_in_dim(grad_matched, start + 6, 1, axis=0)
        given = jnp.concatenate([own, both], axis=0)
        if t:
            given = lax.ppermute(given, "pix", [(p, (p + t) % PARTS) for p in range(PARTS)])
        cotangents.append(given)
    places = jnp.stack([lax.rem(me + PARTS - t, PARTS) for t in range(PARTS)] + [lax.rem(me, 2)])
    partner = [(p, p ^ 1) for p in range(PARTS)]

    everyone = ("pix", "log")

    held = exchange(spread(features, endpoint_owner, endpoint_frame, peers), "log")
    sent, ids = fetch(held, piece, frames, peers)
    maps = unpack(exchange(sent, everyone), piece, peers)
    come = lax.ppermute(maps[SLOTS - 1 :], "pix", partner)
    first = edges(maps, cotangents, places, 0, 2)
    come, first = lax.optimization_barrier((come, first))
    kept, given = shared_edge(maps, come, cotangents, places)
    come = lax.ppermute(given, "pix", partner)
    last = edges(maps, cotangents, places, 2, 1)
    grads = pack(first, last, kept, come, piece, peers)
    sums = land(exchange(grads, everyone), ids, piece, frames)
    return collect(exchange(sums, "log"), frames, piece, peers)


def solution(mesh):
    in_specs = (P("log", "pix", None), P("log", None), P("log", None), P("log", "pix", None))
    out_specs = P("log", "pix", None)
    return jax.shard_map(shards, mesh=mesh, in_specs=in_specs, out_specs=out_specs, check_vma=False)
```

```python
import functools
import math

import jax
import jax.numpy as jnp
from jax import lax
from jax.experimental import pallas as pl
from jax.experimental.pallas import tpu as pltpu
from jax.sharding import PartitionSpec as P

F32 = jnp.float32
BF16 = jnp.bfloat16
LANES = 128
ENDS = 28
PARTS = 4
SLOTS = 7
META = 2
GROUPS = 4


def dot(a, b, ca, cb):
    return lax.dot_general(a, b, (((ca,), (cb,)), ((), ())), preferred_element_type=F32)


def params(mebi):
    return pltpu.CompilerParams(vmem_limit_bytes=mebi * 2**20)


def in_hbm(x):
    return pltpu.with_memory_space_constraint(x, pltpu.HBM)


def vmem():
    return pl.BlockSpec(memory_space=pltpu.VMEM)


def cost(flops, size):
    return pl.CostEstimate(flops=flops, bytes_accessed=size, transcendentals=0)


def spread_kernel(peers, piece, feat_ref, owner_ref, frame_ref, out_ref, wide, line):
    step = pl.program_id(0)
    some = feat_ref.shape[0]
    frames = some * pl.num_programs(0)
    each = piece * some * GROUPS + META
    for f in range(some):
        for k in range(piece):
            block = feat_ref[f, k * peers : (k + 1) * peers, :].astype(F32)
            wide[pl.ds(k * some * GROUPS + step * some + f, peers, stride=each), :] = block

    @pl.when(step == pl.num_programs(0) - 1)
    def _():
        ends = owner_ref.shape[1]
        for at, ref in enumerate((owner_ref, frame_ref)):
            line[...] = jnp.full(line.shape, 127.0, F32)
            line[0:1, 0:ends] = ref[...].astype(F32)
            values = jnp.broadcast_to(line[0:1, :], (peers, LANES))
            wide[pl.ds(each - META + at, peers, stride=each), :] = values
        out_ref[...] = wide[...].astype(BF16)


def spread(features, owners, locals_, peers):
    frames, rows, chans = features.shape
    piece = rows // peers
    total = peers * (piece * frames + META)
    ends = owners.shape[0]
    return pl.pallas_call(
        functools.partial(spread_kernel, peers, piece),
        grid=(GROUPS,),
        out_shape=jax.ShapeDtypeStruct((total, chans), BF16),
        in_specs=[
            pl.BlockSpec((frames // GROUPS, rows, chans), lambda g: (g, 0, 0)),
            pl.BlockSpec((1, ends), lambda g: (0, 0)),
            pl.BlockSpec((1, ends), lambda g: (0, 0)),
        ],
        out_specs=pl.BlockSpec((total, chans), lambda g: (0, 0)),
        scratch_shapes=[pltpu.VMEM((total, chans), F32), pltpu.VMEM((8, LANES), F32)],
        compiler_params=params(12),
        name="spread",
    )(*[in_hbm(x) for x in (features, owners.reshape(1, ends), locals_.reshape(1, ends))])


def lane_of(part, slot):
    odd = part % 2
    own = odd * 6 + slot
    return part // 2 * 14 + jnp.where(slot < 6, own, 12 + odd)


def id_column(owner, frame, part):
    peers = owner.shape[0]
    count = SLOTS * peers
    row = lax.broadcasted_iota(jnp.int32, (count, peers), 0)
    col = lax.broadcasted_iota(jnp.int32, (count, peers), 1)
    pick = jnp.where(lax.rem(row, peers) == col, 1.0, 0.0).astype(BF16)
    every = dot(pick, frame, 1, 0) * peers + dot(pick, owner, 1, 0)
    row = lax.broadcasted_iota(jnp.int32, (count, LANES), 0)
    lane = lax.broadcasted_iota(jnp.int32, (count, LANES), 1)
    mine = lane == lane_of(part, lax.div(row, peers))
    return jnp.sum(jnp.where(mine, every, 0.0), axis=1, keepdims=True)


def id_row(owner, frame, part):
    peers = owner.shape[0]
    count = SLOTS * peers
    row = lax.broadcasted_iota(jnp.int32, (LANES, count), 0)
    col = lax.broadcasted_iota(jnp.int32, (LANES, count), 1)
    pick = jnp.where(row == lane_of(part, lax.div(col, peers)), 1.0, 0.0).astype(BF16)
    every = dot(frame, pick, 1, 0) * peers + dot(owner, pick, 1, 0)
    row = lax.broadcasted_iota(jnp.int32, (peers, count), 0)
    col = lax.broadcasted_iota(jnp.int32, (peers, count), 1)
    return jnp.sum(jnp.where(lax.rem(col, peers) == row, every, 0.0), axis=0, keepdims=True)


def fetch_kernel(piece, frames, peers, held_ref, out_ref, ids_ref, table, held, wide, ready, sems):
    total = peers * frames
    each = piece * SLOTS
    block = peers * each
    pitch = piece * frames + META
    held[...] = held_ref[...].astype(F32)
    for f in range(frames):
        for k in range(piece):
            rows = held[pl.ds(k * frames + f, peers, stride=pitch), :]
            table[f * peers : (f + 1) * peers, k * LANES : (k + 1) * LANES] = rows.astype(BF16)
    for at in range(META):
        ids_ref[at] = held[pl.ds(pitch - META + at, peers, stride=pitch), :].astype(BF16)
    owner, frame = ids_ref[0], ids_ref[1]
    lane = lax.broadcasted_iota(jnp.int32, (SLOTS * peers, total), 1).astype(F32)
    copies = []
    for part in range(PARTS):
        column = id_column(owner, frame, part)
        chosen = jnp.where(column == lane, 1.0, 0.0).astype(BF16)
        rows = dot(chosen, table[...], 1, 0)
        for k in range(piece):
            for s in range(SLOTS):
                some = rows[s * peers : (s + 1) * peers, k * LANES : (k + 1) * LANES]
                wide[part, pl.ds(k * SLOTS + s, peers, stride=each), :] = some
        ready[part] = wide[part].astype(BF16)
        there = out_ref.at[pl.ds(part * block, block)]
        copies.append(pltpu.make_async_copy(ready.at[part], there, sems.at[part]))
        copies[-1].start()
    for copy in copies:
        copy.wait()


def fetch(held, piece, frames, peers):
    block = peers * piece * SLOTS
    return pl.pallas_call(
        functools.partial(fetch_kernel, piece, frames, peers),
        out_shape=(
            pltpu.HBM((PARTS * block, LANES), BF16),
            jax.ShapeDtypeStruct((META, peers, LANES), BF16),
        ),
        in_specs=[vmem()],
        out_specs=(pl.BlockSpec(memory_space=pl.ANY), vmem()),
        scratch_shapes=[
            pltpu.VMEM((peers * frames, piece * LANES), BF16),
            pltpu.VMEM(held.shape, F32),
            pltpu.VMEM((PARTS, block, LANES), F32),
            pltpu.VMEM((PARTS, block, LANES), BF16),
            pltpu.SemaphoreType.DMA((PARTS,)),
        ],
        compiler_params=params(40),
        name="fetch",
    )(held)


def unpack_kernel(piece, peers, in_ref, out_ref, wide):
    each = piece * SLOTS
    wide[...] = in_ref[...].astype(F32)
    for s in range(SLOTS):
        for k in range(piece):
            block = wide[pl.ds(k * SLOTS + s, peers, stride=each), :]
            out_ref[s, k * peers : (k + 1) * peers, :] = block.astype(BF16)


def unpack(got, piece, peers):
    block = peers * piece * SLOTS
    rows = piece * peers
    return pl.pallas_call(
        functools.partial(unpack_kernel, piece, peers),
        grid=(PARTS,),
        out_shape=jax.ShapeDtypeStruct((SLOTS, PARTS * rows, LANES), BF16),
        in_specs=[pl.BlockSpec((block, LANES), lambda p: (p, 0))],
        out_specs=pl.BlockSpec((SLOTS, rows, LANES), lambda p: (0, p, 0)),
        scratch_shapes=[pltpu.VMEM((block, LANES), F32)],
        compiler_params=params(12),
        name="unpack",
    )(got)


def pack_kernel(piece, peers, first_ref, last_ref, kept_ref, come_ref, out_ref, wide):
    each = piece * SLOTS
    for s in range(SLOTS):
        for k in range(piece):
            here = slice(k * peers, (k + 1) * peers)
            if s < 4:
                block = first_ref[s, here, :].astype(F32)
            elif s < 6:
                block = last_ref[s - 4, here, :].astype(F32)
            else:
                block = kept_ref[here, :].astype(F32) + come_ref[here, :].astype(F32)
            wide[pl.ds(k * SLOTS + s, peers, stride=each), :] = block
    out_ref[...] = wide[...].astype(BF16)


def pack(first, last, kept, come, piece, peers):
    block = peers * piece * SLOTS
    rows = piece * peers
    return pl.pallas_call(
        functools.partial(pack_kernel, piece, peers),
        grid=(PARTS,),
        out_shape=jax.ShapeDtypeStruct((PARTS * block, LANES), BF16),
        in_specs=[
            pl.BlockSpec((4, rows, LANES), lambda p: (0, p, 0)),
            pl.BlockSpec((2, rows, LANES), lambda p: (0, p, 0)),
            pl.BlockSpec((rows, LANES), lambda p: (p, 0)),
            pl.BlockSpec((rows, LANES), lambda p: (p, 0)),
        ],
        out_specs=pl.BlockSpec((block, LANES), lambda p: (p, 0)),
        scratch_shapes=[pltpu.VMEM((block, LANES), F32)],
        compiler_params=params(12),
        name="pack",
    )(first, last, kept, come)


def edge_block(q, g, key_all):
    scale = LANES ** (-0.5)
    scores = dot(q, key_all, 1, 1)
    top = jnp.max(scores, axis=1, keepdims=True)
    expo = jnp.exp2((scores - top) * (scale * math.log2(math.e)))
    total = jnp.sum(expo, axis=1, keepdims=True)
    dprobs = dot(g, key_all, 1, 1)
    inverse = 1.0 / total
    probs = expo * inverse
    probs_low = probs.astype(BF16)
    delta = jnp.sum(probs_low.astype(F32) * dprobs, axis=1, keepdims=True)
    dscores = (probs * (dprobs - delta)).astype(BF16)
    grad_query = (dot(dscores, key_all, 1, 0) * scale).astype(BF16)
    grad_keys = dot(q, dscores, 0, 0) * scale + dot(g, probs_low, 0, 0)
    return grad_query, grad_keys


def place_cotangent(place_ref, cot_refs, cot, edge):
    for part in range(PARTS):
        rows = cot_refs[part].shape[1]
        at = pl.multiple_of(place_ref[part] * rows, rows)
        cot[pl.ds(at, rows), :] = cot_refs[part][edge]


def edge_kernel(block, start, count, place_ref, maps_ref, *refs):
    cot_refs = refs[:PARTS]
    out_ref, cots, grad = refs[PARTS:]
    for edge in range(count):
        cot = cots.at[edge]
        place_cotangent(place_ref, cot_refs, cot, start + edge)
        key_all = maps_ref[2 * (start + edge) + 1]
        for step in range(cot.shape[0] // block):
            here = slice(step * block, (step + 1) * block)
            query = maps_ref[2 * (start + edge), here, :]
            grad_query, grad_keys = edge_block(query, cot[here, :], key_all)
            out_ref[2 * edge, here, :] = grad_query
            if step == 0:
                grad[edge] = grad_keys
            else:
                grad[edge] += grad_keys
        out_ref[2 * edge + 1] = grad[edge].T.astype(BF16)


def edges(maps, cotangents, places, start, count):
    _, pixels, chans = maps.shape
    return pl.pallas_call(
        functools.partial(edge_kernel, pixels // 2, start, count),
        in_specs=[pl.BlockSpec(memory_space=pltpu.SMEM)] + [vmem()] * (PARTS + 1),
        out_specs=vmem(),
        out_shape=jax.ShapeDtypeStruct((2 * count, pixels, chans), BF16),
        scratch_shapes=[
            pltpu.VMEM((count, pixels, chans), BF16),
            pltpu.VMEM((count, chans, pixels), F32),
        ],
        compiler_params=params(40),
        cost_estimate=cost(count * 10 * pixels * pixels * chans, count * 5 * pixels * chans * 2),
        name="edges",
    )(places, maps, *cotangents)


def shared_kernel(place_ref, maps_ref, come_ref, *refs):
    cot_refs = refs[:PARTS]
    kept_ref, sent_ref, query, keys, cot, grad = refs[PARTS:]
    pixels = cot.shape[0]
    half = pixels // 2
    odd = place_ref[PARTS]
    place_cotangent(place_ref, cot_refs, cot, cot_refs[0].shape[0] - 1)
    own = maps_ref.at[SLOTS - 1]
    come = come_ref.at[0]

    @pl.when(odd == 0)
    def _():
        query[...] = own[:half, :]
        keys[...] = come[...]

    @pl.when(odd == 1)
    def _():
        query[...] = come[half:, :]
        keys[...] = own[...]

    g = cot[pl.ds(pl.multiple_of(odd * half, half), half), :]
    grad_query, grad_keys = edge_block(query[...], g, keys[...])
    grad[:half, :] = grad_query
    grad[half:, :] = grad_keys.T.astype(BF16)

    @pl.when(odd == 0)
    def _():
        kept_ref[:half, :] = grad[:half, :]
        kept_ref[half:, :] = jnp.zeros((half, LANES), BF16)
        sent_ref[...] = grad[half:, :]

    @pl.when(odd == 1)
    def _():
        sent_ref[:half, :] = jnp.zeros((half, LANES), BF16)
        sent_ref[half:, :] = grad[:half, :]
        kept_ref[...] = grad[half:, :]


def shared_edge(maps, come, cotangents, places):
    _, pixels, chans = maps.shape
    return pl.pallas_call(
        shared_kernel,
        in_specs=[pl.BlockSpec(memory_space=pltpu.SMEM)] + [vmem()] * (PARTS + 2),
        out_specs=[vmem(), vmem()],
        out_shape=[jax.ShapeDtypeStruct((pixels, chans), BF16)] * 2,
        scratch_shapes=[
            pltpu.VMEM((pixels // 2, chans), BF16),
            pltpu.VMEM((pixels, chans), BF16),
            pltpu.VMEM((pixels, chans), BF16),
            pltpu.VMEM((pixels // 2 * 3, chans), BF16),
        ],
        compiler_params=params(40),
        cost_estimate=cost(5 * pixels * pixels * chans, 5 * pixels * chans * 2),
        name="shared_edge",
    )(places, maps, come, *cotangents)


def land_kernel(piece, frames, back_ref, ids_ref, out_ref, values, wide, spread_out):
    peers = ids_ref.shape[1]
    each = piece * SLOTS
    count = SLOTS * peers
    rows = each * peers
    wide[...] = back_ref[...].astype(F32)
    names = []
    for part in range(PARTS):
        names.append(id_row(ids_ref[0], ids_ref[1], part))
        for k in range(piece):
            for s in range(SLOTS):
                block = wide[pl.ds(part * rows + k * SLOTS + s, peers, stride=each), :]
                at = part * count + s * peers
                values[at : at + peers, k * LANES : (k + 1) * LANES] = block.astype(BF16)
    name = jnp.concatenate(names, axis=1)
    some = 4
    for group in range(frames // some):
        every = lax.broadcasted_iota(jnp.int32, (some * peers, PARTS * count), 0) + group * some * peers
        chosen = jnp.where(name == every.astype(F32), 1.0, 0.0).astype(BF16)
        sums = dot(chosen, values[...], 1, 0)
        for f in range(some):
            for k in range(piece):
                block = sums[f * peers : (f + 1) * peers, k * LANES : (k + 1) * LANES]
                at = k * frames + group * some + f
                spread_out[pl.ds(at, peers, stride=piece * frames), :] = block
    out_ref[...] = spread_out[...].astype(BF16)


def land(back, ids, piece, frames):
    peers = ids.shape[1]
    rows = peers * piece * frames
    return pl.pallas_call(
        functools.partial(land_kernel, piece, frames),
        out_shape=jax.ShapeDtypeStruct((rows, LANES), BF16),
        in_specs=[vmem(), vmem()],
        out_specs=vmem(),
        scratch_shapes=[
            pltpu.VMEM((PARTS * SLOTS * peers, piece * LANES), BF16),
            pltpu.VMEM(back.shape, F32),
            pltpu.VMEM((rows, LANES), F32),
        ],
        compiler_params=params(32),
        name="land",
    )(back, ids)


def collect_kernel(piece, peers, back_ref, out_ref, wide):
    step = pl.program_id(0)
    some = out_ref.shape[0]
    frames = some * pl.num_programs(0)
    each = piece * frames

    @pl.when(step == 0)
    def _():
        wide[...] = back_ref[...].astype(F32)

    for f in range(some):
        for k in range(piece):
            block = wide[pl.ds(k * frames + step * some + f, peers, stride=each), :]
            out_ref[f, k * peers : (k + 1) * peers, :] = block


def collect(back, frames, piece, peers):
    return pl.pallas_call(
        functools.partial(collect_kernel, piece, peers),
        grid=(GROUPS,),
        out_shape=jax.ShapeDtypeStruct((frames, piece * peers, LANES), F32),
        in_specs=[vmem()],
        out_specs=pl.BlockSpec((frames // GROUPS, piece * peers, LANES), lambda g: (g, 0, 0)),
        scratch_shapes=[pltpu.VMEM(back.shape, F32)],
        compiler_params=params(16),
        name="collect",
    )(back)


def exchange(blocks, axes):
    total = blocks.shape[0]
    count = lax.axis_size(axes)
    shape = (count, total // count // 2, 2, LANES)
    moved = lax.all_to_all(blocks.reshape(shape), axes, 0, 0, tiled=True)
    return moved.reshape(total, LANES)


def shards(features, endpoint_owner, endpoint_frame, grad_matched):
    peers = lax.axis_size("log")
    frames, rows, chans = features.shape
    piece = rows // peers
    me = lax.axis_index("pix")
    if lax.axis_size("pix") != PARTS or endpoint_owner.shape[0] != ENDS:
        raise ValueError("other sizes")

    cotangents = []
    for t in range(PARTS):
        taker = lax.rem(me + t, PARTS)
        start = lax.div(taker, 2) * 7
        own = lax.dynamic_slice_in_dim(grad_matched, start + lax.rem(taker, 2) * 3, 3, axis=0)
        both = lax.dynamic_slice_in_dim(grad_matched, start + 6, 1, axis=0)
        given = jnp.concatenate([own, both], axis=0)
        if t:
            given = lax.ppermute(given, "pix", [(p, (p + t) % PARTS) for p in range(PARTS)])
        cotangents.append(given)
    places = jnp.stack([lax.rem(me + PARTS - t, PARTS) for t in range(PARTS)] + [lax.rem(me, 2)])
    partner = [(p, p ^ 1) for p in range(PARTS)]

    everyone = ("pix", "log")

    held = exchange(spread(features, endpoint_owner, endpoint_frame, peers), "log")
    sent, ids = fetch(held, piece, frames, peers)
    maps = unpack(exchange(sent, everyone), piece, peers)
    come = lax.ppermute(maps[SLOTS - 1 :], "pix", partner)
    first = edges(maps, cotangents, places, 0, 2)
    come, first = lax.optimization_barrier((come, first))
    kept, given = shared_edge(maps, come, cotangents, places)
    come = lax.ppermute(given, "pix", partner)
    last = edges(maps, cotangents, places, 2, 1)
    grads = pack(first, last, kept, come, piece, peers)
    sums = land(exchange(grads, everyone), ids, piece, frames)
    return collect(exchange(sums, "log"), frames, piece, peers)


def solution(mesh):
    in_specs = (P("log", "pix", None), P("log", None), P("log", None), P("log", "pix", None))
    out_specs = P("log", "pix", None)
    return jax.shard_map(shards, mesh=mesh, in_specs=in_specs, out_specs=out_specs, check_vma=False)
```
